256 devices in a mesh: ctx: 32 (over z, x), exp: 8 (over y, core).
Axes of the slice: x: 4, y: 4, z: 8, core: 2. Of those that a mesh axis runs over, the one named last changes fastest.
Arguments:
- queries: bfloat16 [16, 2, 128, 576], P('exp'), may hold values from -300 to 300
- new_latent: bfloat16 [16, 2, 576], P('exp'), may hold values from -8 to 8
- cache: bfloat16 [16, 16384, 576], P('exp', 'ctx'), may hold values from -6 to 6
- lengths: int32 [16], P('exp'), may hold values from 4096 to 16384, as said below
- value_up: bfloat16 [128, 512, 128], P('ctx'), may hold values from -1 to 1
- out_proj: bfloat16 [16384, 7168], P(('ctx', 'exp')), may hold values from -0.046875 to 0.046875
- residual: bfloat16 [16, 2, 7168], P('exp', None, 'ctx'), may hold values from -9 to 9
- norm_gain: float32 [7168], P('ctx'), may hold values from 0.1 to 1.9
- route_ids: int32 [16, 2, 8], P('exp'), may hold values from 0 to 15, all different within a row; in each aligned block of 4 rows (0 to 3, 4 to 7, ..., all dimensions but the last counted through in order) at most 4 rows name the same one
- route_weights: float32 [16, 2, 8], P('exp'), may hold values from 0.05 to 0.5
- gate_up: bfloat16 [16, 7168, 4096], P('exp', 'ctx'), may hold values from -0.0625 to 0.0625
- expert_down: bfloat16 [16, 2048, 7168], P('exp', None, 'ctx'), may hold values from -0.125 to 0.125
Outputs:
- mixed: bfloat16 [16, 2, 7168], P('exp', None, 'ctx')
The draws below stay inside these ranges and needn't reach their ends.
Inputs may be any that keep to these rules, and one draw needn't show every extreme that they name: `lengths`: some sequence has all 16384 positions cached. `route_ids`: each token names 8 different experts; on the tokens of one index of exp some expert is named by all 4 of them.
All inputs are finite; a program needn't handle non-finite values.
Results may differ from the reference program's by a relative error of at most 0.025.
Values may be sent and summed in bfloat16 or wider, within the bound.
A program may use at most 128 MiB of HBM per device.

```python
import math
import jax
import jax.numpy as jnp
import numpy as np
from jax import lax

D = 7168
HEADS = 128
LATENT = 512
ROPE = 64
VDIM = 128
FFE = 2048
TOPK = 8
STEPS = 2
ROWS = 16
CTX = 16384
TOK = 4
EXPERTS = 16


def query_base(key):
    noise = jax.random.normal(jax.random.fold_in(key, 101), (ROWS, STEPS, HEADS, LATENT + ROPE), jnp.float32)
    return jnp.clip(noise, -6.0, 6.0)


def draw_queries(key, part):
    base = query_base(key)
    return base.astype(jnp.bfloat16)


def draw_new_latent(key, part):
    base = query_base(key)
    fresh = 1.2 / math.sqrt(HEADS) * jnp.sum(base, axis=2)
    return jnp.clip(fresh, -8.0, 8.0).astype(jnp.bfloat16)


def draw_cache(key, part):
    key = jax.random.fold_in(key, 3)
    values = jnp.clip(jax.random.normal(key, (ROWS, CTX, LATENT + ROPE), jnp.float32), -6.0, 6.0)
    return values.astype(jnp.bfloat16)


def draw_lengths(key, part):
    key = jax.random.fold_in(key, 4)
    counts = jax.random.randint(key, (ROWS,), CTX // 4, CTX + 1, dtype=jnp.int32)
    chosen = jax.random.randint(jax.random.fold_in(key, 5), (), 0, ROWS, dtype=jnp.int32)
    return counts.at[chosen].set(CTX)


def draw_residual(key, part):
    key = jax.random.fold_in(key, 6)
    column = jnp.arange(D, dtype=jnp.float32) / D
    rough = jax.random.uniform(jax.random.fold_in(key, 7), (D,), jnp.float32, 0.5, 1.5)
    values = jnp.clip(jax.random.normal(key, (ROWS, STEPS, D), jnp.float32), -6.0, 6.0)
    values = 0.06 * values * jnp.exp(math.log(3.0) * column) * rough
    return jnp.clip(values, -9.0, 9.0).astype(jnp.bfloat16)


def steps_of(stream_key, extent, cuts, least, largest):
    gain, own = 1.0, jax.random.fold_in(stream_key, 6)
    for position, blocks in cuts:
        heights = jnp.exp(jax.random.uniform(jax.random.fold_in(own, position), (blocks,), jnp.float32, least / len(cuts), largest / len(cuts)))
        gain = gain * jnp.repeat(heights, extent[position] // blocks).reshape([-1 if axis == position else 1 for axis in range(len(extent))])
    return gain


def shared_out(rng, own, number, rows, amount, top, most, lean):
    ranking = jax.random.permutation(rng, amount)
    crowded, ordinary = load_shares(amount, rows * top, most, lean, True), load_shares(amount, rows * top, most, lean, False)
    places = jnp.arange(amount)

    def named(sizes, rotation):
        used = int((sizes > 0).sum())
        fixed = max(1, used // 4)
        shifted = fixed + (places - fixed + rotation * (used - fixed)) % max(1, amount - fixed)
        return jnp.zeros((amount,), jnp.int32).at[ranking[jnp.where(places < fixed, places, shifted)]].set(jnp.asarray(sizes, jnp.int32))

    sizes = jnp.where(number % 4 == 0, named(crowded, number // 4), named(ordinary, number - number // 4 - 1))
    mixed = jax.random.permutation(jax.random.fold_in(own, 3), amount)
    giver, receiver = mixed[0:amount // 2 * 2:2], mixed[1:amount // 2 * 2:2]
    room = jnp.minimum(sizes[giver] - 1, most - sizes[receiver]) // 2
    room = jnp.where((giver == ranking[0]) | (receiver == ranking[0]) | (sizes[receiver] == 0), 0, jnp.maximum(room, 0))
    shifted = jax.random.randint(jax.random.fold_in(own, 4), (amount // 2,), 0, 1 << 20) % (room + 1)
    sizes = sizes.at[giver].add(-shifted).at[receiver].add(shifted)
    items = jnp.searchsorted(jnp.cumsum(sizes), jnp.arange(rows * top), side="right").astype(jnp.int32)
    table = items.reshape(top, rows).T
    table = table[jax.random.permutation(jax.random.fold_in(own, 1), rows)]
    rotation = jax.random.randint(jax.random.fold_in(own, 2), (rows, 1), 0, top)
    return jnp.take_along_axis(table, (jnp.arange(top)[None, :] + rotation) % top, axis=1)


def load_shares(number_of, total, reach, slope, full):
    weights = [(1 << 20) // math.isqrt(standing ** slope) + 1 for standing in range(1, number_of + 1)]
    largest = reach if full else min(reach, max(-(-total // number_of), total * weights[0] // sum(weights)))
    least = 1 if total - largest >= number_of - 1 else 0
    given, surplus = [largest] + [least] * (number_of - 1), total - largest - least * (number_of - 1)
    while surplus > 0:
        free = [i for i in range(1, number_of) if given[i] < largest] or [i for i in range(1, number_of) if given[i] < reach]
        whole, budget = sum([weights[i] for i in free]), surplus
        for i in free:
            more = min(reach - given[i], max(1, budget * weights[i] // whole), surplus)
            given[i] = given[i] + more
            surplus = surplus - more
    return np.array(given)


def bell_draw(own_key, extent, spread, bound, split=(), kind=jnp.bfloat16):
    values = jax.random.normal(own_key, extent, jnp.float32) * spread
    if len(split) > 0:
        values = steps_of(own_key, extent, split, -0.22, 0.18) * values
    return jnp.clip(values, min=-bound, max=bound).astype(kind)


def setup_inputs(seed: int = 0) -> dict:
    key_of = jax.random.split(jax.random.key(seed), 13)
    queries = draw_queries(jax.random.fold_in(key_of[12], 71), 0)
    new_latent = draw_new_latent(jax.random.fold_in(key_of[12], 71), 0)
    cache = draw_cache(jax.random.fold_in(key_of[12], 71), 0)
    lengths = draw_lengths(jax.random.fold_in(key_of[12], 71), 0)
    value_up = bell_draw(key_of[4], (HEADS, LATENT, VDIM), (LATENT // 16) ** -0.5, 1.0, ((0, 32),))
    out_proj = bell_draw(key_of[5], (HEADS * VDIM, D), (HEADS * VDIM) ** -0.5, 0.046875, ((0, 256),))
    residual = draw_residual(jax.random.fold_in(key_of[12], 71), 0)
    norm_gain = jnp.clip(1.0 + 0.18 * jax.random.normal(key_of[7], (D,), jnp.float32), 0.1, 1.9)
    route_ids_keys = jax.random.split(jax.random.fold_in(key_of[8], 1), ROWS * STEPS // TOK)
    route_ids_turns = jax.random.permutation(jax.random.fold_in(key_of[8], 3), ROWS * STEPS // TOK)
    route_ids = jax.vmap(lambda own, number: shared_out(jax.random.fold_in(key_of[8], 2), own, number, TOK, EXPERTS, TOPK, TOK, 2))(route_ids_keys, route_ids_turns).reshape((ROWS, STEPS, TOPK))
    route_weights = jnp.clip(jnp.exp(math.log(0.5) - 2.3025851 * jax.random.uniform(key_of[9], (ROWS, STEPS, TOPK), jnp.float32) ** steps_of(key_of[9], (ROWS, STEPS, TOPK), ((0, 8),), -0.2, 0.2)), 0.05, 0.5)
    gate_up = bell_draw(key_of[10], (EXPERTS, D, 2 * FFE), D ** -0.5, 0.0625, ((0, 8), (1, 32)))
    expert_down = bell_draw(key_of[11], (EXPERTS, FFE, D), FFE ** -0.5, 0.125, ((0, 8), (2, 32)))
    return dict(queries=queries, new_latent=new_latent, cache=cache, lengths=lengths, value_up=value_up, out_proj=out_proj, residual=residual, norm_gain=norm_gain, route_ids=route_ids, route_weights=route_weights, gate_up=gate_up, expert_down=expert_down)


qk_scale = 1.0 / math.sqrt(192.0)
norm_eps = 1e-06

def attend_row(packed):
    row_query, row_fresh, row_keys, row_length = packed
    flat_query = row_query.reshape(STEPS * HEADS, LATENT + ROPE)
    scores = jnp.dot(flat_query, row_keys.T, preferred_element_type=jnp.float32) * qk_scale
    visible = jnp.arange(CTX) < row_length
    scores = jnp.where(visible[None, :], scores, -jnp.inf)
    fresh_scores = jnp.dot(flat_query, row_fresh.T, preferred_element_type=jnp.float32) * qk_scale
    step_of = jnp.arange(STEPS * HEADS) // HEADS
    causal = jnp.arange(STEPS)[None, :] <= step_of[:, None]
    fresh_scores = jnp.where(causal, fresh_scores, -jnp.inf)
    peak_score = jnp.maximum(lax.optimization_barrier(jnp.max(scores, axis=1)), lax.optimization_barrier(jnp.max(fresh_scores, axis=1)))
    weights = jnp.exp(scores - peak_score[:, None])
    fresh_weights = jnp.exp(fresh_scores - peak_score[:, None])
    denom = lax.optimization_barrier(jnp.sum(weights, axis=1)) + lax.optimization_barrier(jnp.sum(fresh_weights, axis=1))
    mixture = jnp.dot(weights.astype(jnp.bfloat16), row_keys[:, :LATENT], preferred_element_type=jnp.float32)
    mixture = mixture + jnp.dot(fresh_weights.astype(jnp.bfloat16), row_fresh[:, :LATENT], preferred_element_type=jnp.float32)
    return (mixture / denom[:, None]).reshape(STEPS, HEADS, LATENT)

def reference(queries, new_latent, cache, lengths, value_up, out_proj, residual, norm_gain, route_ids, route_weights, gate_up, expert_down):
    tok_total = ROWS * STEPS
    latent_out = lax.map(attend_row, (queries, new_latent, cache, lengths))
    values = jnp.einsum('rshl,hlv->rshv', latent_out, value_up.astype(jnp.float32), precision=lax.Precision.HIGHEST).astype(jnp.bfloat16)
    flat_values = values.reshape(tok_total, HEADS * VDIM)
    attn_out = jnp.dot(flat_values, out_proj, preferred_element_type=jnp.float32)
    hidden = (residual.reshape(tok_total, D).astype(jnp.float32) + attn_out).astype(jnp.bfloat16)
    hidden_f = hidden.astype(jnp.float32)
    squares = lax.optimization_barrier(jnp.sum(hidden_f * hidden_f, axis=1))
    normed = (hidden_f * lax.rsqrt(squares / D + norm_eps)[:, None] * norm_gain[None, :]).astype(jnp.bfloat16)
    route_list = route_ids.reshape(tok_total, TOPK)
    route_coef = route_weights.reshape(tok_total, TOPK)
    expert_grid = jnp.arange(EXPERTS, dtype=jnp.int32)
    matches = (route_list[:, :, None] == expert_grid[None, None, :]).astype(jnp.float32)
    dense = lax.optimization_barrier(jnp.sum(route_coef[:, :, None] * matches, axis=1))

    def add_expert(running, packed):
        proj_in, proj_out, mix_coef = packed
        both = jnp.dot(normed, proj_in, preferred_element_type=jnp.float32)
        activated = (jax.nn.silu(both[:, :FFE]) * both[:, FFE:]).astype(jnp.bfloat16)
        expert_out = jnp.dot(activated, proj_out, preferred_element_type=jnp.float32).astype(jnp.bfloat16)
        return (running + mix_coef[:, None] * expert_out.astype(jnp.float32), None)
    routed, unused = lax.scan(add_expert, jnp.zeros((tok_total, D), jnp.float32), (gate_up, expert_down, dense.T))
    mixed = (hidden_f + routed).astype(jnp.bfloat16)
    return mixed.reshape(ROWS, STEPS, D)
```

```python
import functools
import math

import jax
import jax.numpy as jnp
from jax import lax
from jax.experimental import pallas as pl
from jax.experimental.pallas import tpu as pltpu
from jax.sharding import PartitionSpec as P

STEPS = 2
LATENT = 512
VDIM = 128
TOPK = 8
CHIPS_X = 4
LANES = 128

qk_scale = 1.0 / math.sqrt(192.0)
norm_eps = 1e-06
MESH = pl.DeviceIdType.MESH
F32 = jnp.float32
BF16 = jnp.bfloat16
HIGH = lax.Precision.HIGHEST


def iota(shape, dim):
    return lax.broadcasted_iota(jnp.int32, shape, dim)


def log2(n):
    assert n & (n - 1) == 0
    return n.bit_length() - 1


def mm(a, b, precision=None):
    return jnp.dot(a, b, preferred_element_type=F32, precision=precision)


def mm_nt(a, b):
    return lax.dot_general(a, b, (((1,), (1,)), ((), ())), preferred_element_type=F32)


def far_first(n):
    return sorted(range(1, n), key=lambda k: (-min(k, n - k), k))


def pad_lanes(a, width):
    return jnp.concatenate([a, jnp.zeros((a.shape[0], width - a.shape[1]), a.dtype)], axis=1)


def pad_rows(a, height):
    return jnp.concatenate([a, jnp.zeros((height - a.shape[0], a.shape[1]), a.dtype)], axis=0)


class Plan:
    def __init__(self, nx, nz, ne, queries, cache, out_proj, gate_up):
        self.nx, self.nz, self.ne = nx, nz, ne
        self.rows = queries.shape[0]
        self.heads = queries.shape[2]
        self.width = queries.shape[3]
        self.span = cache.shape[1]
        self.hl = self.heads // (nx * nz)
        self.tok = self.rows * STEPS
        self.block = self.tok * self.hl
        self.total = self.tok * ne
        self.model = out_proj.shape[1]
        self.feat = self.model // (nx * nz)
        self.featp = -(-self.feat // LANES) * LANES
        self.vrows = out_proj.shape[0]
        self.ffe = gate_up.shape[2] // 2
        self.experts = gate_up.shape[0]
        self.nzz = nz // self.experts
        self.fb = self.ffe // (nx * self.nzz)
        self.base, at = {}, 0
        for name, n in (
            ("res", ne - 1),
            ("ax", nx - 1),
            ("axs", nx - 1),
            ("az", nz - 1),
            ("azs", nz - 1),
            ("b", ne - 1),
            ("core", nx),
            ("cx", nx - 1),
            ("cz", nz - 1),
            ("ce", ne - 1),
            ("sx", nx - 1),
            ("sz", nz - 1),
            ("ex", nx - 1),
            ("ez", nz - 1),
            ("gz", nz - 1),
            ("gx", nx - 1),
            ("f", ne - 1),
        ):
            self.base[name] = at
            at += n
        self.n_remote = at
        self.n_local = 2 * self.rows + 3 + self.experts * 2 * nx


def joined(stats):
    top = functools.reduce(jnp.maximum, [s[0:1, :] for s in stats])
    raw = [s[1:2, :] * jnp.exp(s[0:1, :] - top) for s in stats]
    total = functools.reduce(jnp.add, raw)
    inv = jnp.where(total > 0.0, 1.0 / jnp.where(total > 0.0, total, 1.0), 0.0)
    coefs = [r * inv for r in raw]
    width = top.shape[1]
    sub = iota((8, width), 0)
    packed = jnp.zeros((8, width), F32)
    for k, c in enumerate(coefs):
        packed = jnp.where(sub == k, c, packed)
    columns = jnp.transpose(pad_rows(packed, LANES))
    both = jnp.where(sub == 0, top, jnp.where(sub == 1, total, 0.0))
    return columns, both


def kernel(
    pn,
    q_hbm,
    nl_ref,
    cache_hbm,
    len_ref,
    vu_hbm,
    op_hbm,
    res_ref,
    gain_ref,
    ids_ref,
    rw_ref,
    gu_hbm,
    dn_hbm,
    out_ref,
    qs,
    ks,
    vus,
    ops,
    gus,
    dns,
    opw,
    rb,
    ra,
    os_,
    oxr,
    sxs,
    sxr,
    ozs,
    ozr,
    szs,
    szr,
    ctx_cols,
    ctz_cols,
    vs,
    vr,
    cs,
    cr,
    xs,
    xr,
    zs,
    zr,
    ys,
    yr,
    qxs,
    qxr,
    qzs,
    qzr,
    es,
    exr,
    ezs,
    ezr,
    act,
    fs,
    fr,
    send_sems,
    recv_sems,
    local_sems,
):
    nx, nz, ne = pn.nx, pn.nz, pn.ne
    ctx = lax.axis_index("ctx")
    me = lax.axis_index("exp")
    my_z, my_x = ctx // nx, lax.rem(ctx, nx)
    core = lax.rem(me, 2)
    pending = []

    def x_of(k):
        return lax.rem(my_x + k, nx)

    def z_of(k):
        return lax.rem(my_z + k, nz)

    def e_of(k):
        return lax.rem(me + k, ne)

    def x_dev(k):
        return (my_z * nx + x_of(k), me)

    def z_dev(k):
        return (z_of(k) * nx + my_x, me)

    def e_dev(k):
        return (ctx, e_of(k))

    core_dev = (ctx, me + 1 - 2 * core)

    def remote(src, dst, name, slot, dev):
        at = pn.base[name] + slot
        return pltpu.make_async_remote_copy(
            src_ref=src,
            dst_ref=dst,
            send_sem=send_sems.at[at],
            recv_sem=recv_sems.at[at],
            device_id=dev,
            device_id_type=MESH,
        )

    def send(src, dst, name, slot, dev):
        copy = remote(src, dst, name, slot, dev)
        copy.start()
        pending.append(copy)

    def receive(dst, name, slot, dev):
        remote(dst, dst, name, slot, dev).wait_recv()

    local_at = [0]

    def local(src, dst):
        copy = pltpu.make_async_copy(src, dst, local_sems.at[local_at[0]])
        local_at[0] += 1
        copy.start()
        return copy

    q_copies = [local(q_hbm.at[r], qs.at[r]) for r in range(pn.rows)]
    k_copies = [
        local(cache_hbm.at[r], ks.at[r, :, pl.ds(0, pn.span)]) for r in range(pn.rows)
    ]

    barrier = pltpu.get_barrier_semaphore()
    peers = (
        [x_dev(k) for k in range(1, nx)]
        + [z_dev(k) for k in range(1, nz)]
        + [e_dev(k) for k in range(1, ne)]
    )
    for dev in peers:
        pl.semaphore_signal(barrier, inc=1, device_id=dev, device_id_type=MESH)

    for r in range(pn.rows):
        fresh = pad_lanes(nl_ref[r].astype(F32), -(-pn.width // LANES) * LANES)
        fresh = jnp.transpose(pad_rows(fresh, LANES))[0 : pn.width, :]
        ks[r, :, pl.ds(pn.span, LANES)] = fresh.astype(BF16)
    res_rows = jnp.concatenate([res_ref[r].astype(F32) for r in range(pn.rows)], axis=0)
    rb[...] = pad_rows(pad_lanes(res_rows, pn.featp), 16).astype(BF16)
    ra[me] = rb[...]

    qrows = STEPS * pn.heads
    keys = pn.span + LANES
    m = iota((qrows, qrows), 0)
    lh, lz = log2(pn.hl), log2(nz)
    m_head = m & (pn.hl - 1)
    m_step = (m >> lh) & (STEPS - 1)
    m_z = (m >> (lh + 1)) & (nz - 1)
    m_x = m >> (lh + 1 + lz)
    source = m_step * pn.heads + (m_z * nx + m_x) * pn.hl + m_head
    perm = jnp.where(iota((qrows, qrows), 1) == source, 1.0, 0.0).astype(BF16)

    col = iota((qrows, keys), 1)
    step = (iota((qrows, keys), 0) >> lh) & (STEPS - 1)
    first = jnp.where(ctx == 0, 0, -LANES)
    is_fresh = (col >= pn.span) & (col - pn.span <= step + first)
    position = ctx * pn.span + col

    weight_copies = {}
    partial, peaks, denoms = [], [], []
    for r in range(pn.rows):
        q_copies[r].wait()
        k_copies[r].wait()
        if r == pn.rows - 1:
            weight_copies["vu"] = local(vu_hbm, vus)
            weight_copies["op"] = local(op_hbm, ops)
            for x in range(nx):
                for j in range(pn.experts):
                    for g in range(2):
                        at = g * pn.ffe + x * pn.nzz * pn.fb
                        weight_copies["gu", x, j, g] = local(
                            gu_hbm.at[j, :, pl.ds(at, pn.nzz * pn.fb)], gus.at[x, j, g]
                        )
            weight_copies["dn"] = local(dn_hbm, dns)
        qp = functools.reduce(
            jnp.add,
            [
                mm_nt(perm[:, s * pn.heads : (s + 1) * pn.heads], qs[r, s])
                for s in range(STEPS)
            ],
        ).astype(BF16)
        scores = mm(qp, ks[r])
        visible = ((col < pn.span) & (position < len_ref[r])) | is_fresh
        scores = jnp.where(visible, scores * qk_scale, -1e30)
        peak = jnp.max(scores, axis=1, keepdims=True)
        weights = jnp.where(visible, jnp.exp(scores - peak), 0.0)
        denom = jnp.sum(weights, axis=1, keepdims=True)
        mixture = mm_nt(weights.astype(BF16), ks[r, pl.ds(0, LATENT), :])
        inv = jnp.where(denom > 0.0, 1.0 / jnp.where(denom > 0.0, denom, 1.0), 0.0)
        partial.append(mixture * inv)
        peaks.append(peak)
        denoms.append(denom)

    pl.semaphore_wait(barrier, len(peers))

    half = STEPS * pn.hl
    groups = nx * nz
    merged = jnp.concatenate([p.reshape(groups, half, LATENT) for p in partial], axis=1)
    os_[...] = merged.astype(BF16).reshape(nx, nz, pn.block, LATENT)
    lane = iota((qrows, LANES), 1)
    stat = [
        jnp.where(lane == 0, p, jnp.where(lane == 1, d, 0.0)) for p, d in zip(peaks, denoms)
    ]
    stat = jnp.concatenate([s.reshape(groups, half, LANES) for s in stat], axis=1)
    stat = stat.reshape(nx, nz * pn.block, LANES)
    for x in range(nx):
        sxs[x] = jnp.transpose(stat[x])[0:8, :]
    for k in far_first(nx):
        xp = x_of(k)
        send(sxs.at[xp], sxr.at[k - 1], "axs", k - 1, x_dev(k))
        send(os_.at[xp], oxr.at[k - 1], "ax", k - 1, x_dev(k))
    for k in range(1, ne):
        send(rb, ra.at[me], "res", k - 1, e_dev(k))

    weight_copies["op"].wait()
    for z in range(nz):
        for x in range(nx):
            c = z * nx + x
            piece = ops[:, c * pn.feat : (c + 1) * pn.feat]
            opw[x, :, z * pn.featp : (z + 1) * pn.featp] = pad_lanes(piece, pn.featp)

    for k in range(1, nx):
        receive(sxr.at[k - 1], "axs", k - 1, x_dev(k))
    columns, both = joined([sxs[my_x]] + [sxr[k - 1] for k in range(1, nx)])
    ctx_cols[...] = columns
    szs[...] = both
    for k in range(1, nx):
        receive(oxr.at[k - 1], "ax", k - 1, x_dev(k))
    for k in far_first(nz) + [0]:
        zp = z_of(k)
        cols = ctx_cols[pl.ds(pl.multiple_of(zp * pn.block, pn.block), pn.block), :]
        acc = cols[:, 0:1] * os_[my_x, zp].astype(F32)
        for i in range(1, nx):
            acc = acc + cols[:, i : i + 1] * oxr[i - 1, zp].astype(F32)
        ozs[zp] = acc.astype(BF16)
        if k > 0:
            send(szs, szr.at[k - 1], "azs", k - 1, z_dev(k))
            send(ozs.at[zp], ozr.at[k - 1], "az", k - 1, z_dev(k))

    for k in range(1, ne):
        receive(ra.at[e_of(ne - k)], "res", k - 1, e_dev(k))
    lt, ly = log2(pn.tok), log2(ne // 2)

    def owner_of(n):
        y = (n >> lt) & (ne // 2 - 1)
        return 2 * y + (n >> (lt + ly)), n & (pn.tok - 1)

    n_row = iota((pn.total, ne * 16), 0)
    n_owner, n_tok = owner_of(n_row)
    spread = iota((pn.total, ne * 16), 1)
    pick = jnp.where(spread == n_owner * 16 + n_tok, 1.0, 0.0).astype(BF16)
    residual = mm(pick, ra[...].reshape(ne * 16, pn.featp))
    weight_copies["vu"].wait()

    for k in range(1, nz):
        receive(szr.at[k - 1], "azs", k - 1, z_dev(k))
    columns, _ = joined([szs[...]] + [szr[k - 1] for k in range(1, nz)])
    ctz_cols[...] = columns
    cols = ctz_cols[pl.ds(pl.multiple_of(my_z * pn.block, pn.block), pn.block), :]
    acc = cols[:, 0:1] * ozs[my_z].astype(F32)
    for k in range(1, nz):
        receive(ozr.at[k - 1], "az", k - 1, z_dev(k))
        acc = acc + cols[:, k : k + 1] * ozr[k - 1].astype(F32)
    latent_out = acc.astype(BF16)

    for i in range(pn.hl):
        vs[i] = mm(latent_out, vus[i]).astype(BF16)
    per_head = ne // pn.hl
    for k in range(1, ne):
        send(vs.at[e_of(k) // per_head], vr.at[me], "b", k - 1, e_dev(k))
    vr[me] = vs[me // per_head]
    place = n_tok * pn.hl + me // per_head
    value_pick = jnp.where(spread == n_owner * 16 + place, 1.0, 0.0).astype(BF16)
    for k in range(1, ne):
        receive(vr.at[e_of(ne - k)], "b", k - 1, e_dev(k))
    picked = mm(value_pick, vr[...].reshape(ne * 16, VDIM))
    values = picked[:, 0 : pn.vrows]
    for part in range(1, per_head):
        at = part * pn.vrows
        values = jnp.where(
            lax.rem(me, per_head) == part, picked[:, at : at + pn.vrows], values
        )
    values = values.astype(BF16)

    order = far_first(nx) + [0]
    hr = pn.total // 2
    for k in order:
        part = mm(values, opw[x_of(k)]).astype(BF16)
        cs[k, 0] = part[0:hr, :]
        cs[k, 1] = part[hr:, :]
        send(cs.at[k, 1 - core], cr.at[k], "core", k, core_dev)
    for k in order:
        receive(cr.at[k], "core", k, core_dev)
        for z in range(nz):
            at = slice(z * pn.featp, (z + 1) * pn.featp)
            xs[k, z] = (cs[k, core, :, at].astype(F32) + cr[k, :, at].astype(F32)).astype(BF16)
        if k > 0:
            send(xs.at[k], xr.at[k - 1], "cx", k - 1, x_dev(k))
    for k in range(1, nx):
        receive(xr.at[k - 1], "cx", k - 1, x_dev(k))
    for k in far_first(nz) + [0]:
        zp = z_of(k)
        acc = xs[0, zp].astype(F32)
        for i in range(1, nx):
            acc = acc + xr[i - 1, zp].astype(F32)
        zs[zp] = acc.astype(BF16)
        if k > 0:
            send(zs.at[zp], zr.at[k - 1], "cz", k - 1, z_dev(k))
    acc = zs[my_z].astype(F32)
    for k in range(1, nz):
        receive(zr.at[k - 1], "cz", k - 1, z_dev(k))
        acc = acc + zr[k - 1].astype(F32)
    ys[...] = acc.astype(BF16)
    yr[me] = ys[...]
    for k in range(1, ne):
        send(ys, yr.at[me], "ce", k - 1, e_dev(k))
    for k in range(1, ne):
        receive(yr.at[e_of(ne - k)], "ce", k - 1, e_dev(k))
    sides = []
    for c in range(2):
        acc = yr[c].astype(F32)
        for y in range(1, ne // 2):
            acc = acc + yr[2 * y + c].astype(F32)
        sides.append(acc)
    hidden = (residual + jnp.concatenate(sides, axis=0)).astype(BF16)
    hidden_f = hidden.astype(F32)

    squares = jnp.sum(hidden_f * hidden_f, axis=1, keepdims=True)
    squares = pad_rows(jnp.broadcast_to(squares, (pn.total, LANES)), LANES)
    qxs[...] = jnp.transpose(squares)[0:8, :]
    for k in far_first(nx):
        send(qxs, qxr.at[k - 1], "sx", k - 1, x_dev(k))
    scaled = (hidden_f[:, 0 : pn.feat] * gain_ref[...].reshape(1, pn.feat)).astype(BF16)
    for copy in [weight_copies[key] for key in weight_copies if key[0] == "gu"]:
        copy.wait()
    fb = pn.fb
    for k in order:
        xp = x_of(k)
        for j in range(pn.experts):
            for g in range(2):
                part = mm(scaled, gus[xp, j, g]).astype(BF16)
                for zz in range(pn.nzz):
                    es[k, j * pn.nzz + zz, :, g * fb : (g + 1) * fb] = part[
                        :, zz * fb : (zz + 1) * fb
                    ]
        if k > 0:
            send(es.at[k], exr.at[k - 1], "ex", k - 1, x_dev(k))
    acc = qxs[...]
    for k in range(1, nx):
        receive(qxr.at[k - 1], "sx", k - 1, x_dev(k))
        acc = acc + qxr[k - 1]
    qzs[...] = acc
    for k in far_first(nz):
        send(qzs, qzr.at[k - 1], "sz", k - 1, z_dev(k))
    for k in range(1, nx):
        receive(exr.at[k - 1], "ex", k - 1, x_dev(k))
    for k in far_first(nz) + [0]:
        zp = z_of(k)
        acc = es[0, zp].astype(F32)
        for i in range(1, nx):
            acc = acc + exr[i - 1, zp].astype(F32)
        ezs[zp] = acc.astype(BF16)
        if k > 0:
            send(ezs.at[zp], ezr.at[k - 1], "ez", k - 1, z_dev(k))
    acc = qzs[...]
    for k in range(1, nz):
        receive(qzr.at[k - 1], "sz", k - 1, z_dev(k))
        acc = acc + qzr[k - 1]
    scale_row = lax.rsqrt(acc / pn.model + norm_eps)
    scale = jnp.transpose(pad_rows(scale_row, LANES))[0 : pn.total, 0:1]
    acc = ezs[my_z].astype(F32)
    for k in range(1, nz):
        receive(ezr.at[k - 1], "ez", k - 1, z_dev(k))
        acc = acc + ezr[k - 1].astype(F32)
    acc = acc * scale
    gate, up = acc[:, 0:fb], acc[:, fb : 2 * fb]
    activated = gate / (1.0 + jnp.exp(-gate)) * up
    act[my_x, my_z] = activated.astype(BF16)

    for k in far_first(nz):
        send(act.at[my_x, my_z], act.at[my_x, my_z], "gz", k - 1, z_dev(k))
    weight_copies["dn"].wait()
    for k in range(1, nz):
        receive(act.at[my_x, z_of(nz - k)], "gz", k - 1, z_dev(k))
    for k in far_first(nx):
        send(act.at[my_x], act.at[my_x], "gx", k - 1, x_dev(k))
    depth = pn.nzz * fb
    outs = [jnp.zeros((pn.total, pn.feat), F32) for _ in range(pn.experts)]
    for k in range(nx):
        xp = x_of(nx - k)
        if k > 0:
            receive(act.at[xp], "gx", k - 1, x_dev(k))
        for j in range(pn.experts):
            rows = jnp.concatenate(
                [act[xp, j * pn.nzz + zz] for zz in range(pn.nzz)], axis=1
            )
            down = dns[j, :, pl.ds(pl.multiple_of(xp * depth, depth), depth)]
            outs[j] = outs[j] + mm_nt(rows, down)

    s_row = iota((ne * 16, pn.total), 0)
    s_owner, s_tok = owner_of(iota((ne * 16, pn.total), 1))
    acc = jnp.zeros((ne * 16, pn.featp), F32)
    for j in range(pn.experts):
        put = jnp.where(s_row == s_owner * 16 + j * pn.tok + s_tok, 1.0, 0.0).astype(BF16)
        acc = acc + mm(put, pad_lanes(outs[j], pn.featp).astype(BF16))
    fs[...] = acc.astype(BF16).reshape(ne, 16, pn.featp)
    for k in range(1, ne):
        send(fs.at[e_of(k)], fr.at[me], "f", k - 1, e_dev(k))
    fr[me] = fs[me]

    ids = pad_rows(
        jnp.concatenate([ids_ref[r] for r in range(pn.rows)], axis=0), 8
    )
    coef = pad_rows(jnp.concatenate([rw_ref[r] for r in range(pn.rows)], axis=0), 8)
    c_row, c_col = iota((8, ne * 16), 0), iota((8, ne * 16), 1)
    place = c_col & 15
    expert = (c_col >> 4) * pn.experts + (place >> lt)
    used = (place < pn.experts * pn.tok) & ((place & (pn.tok - 1)) == c_row)
    mix = jnp.zeros((8, ne * 16), F32)
    for t in range(TOPK):
        mix = mix + jnp.where(used & (expert == ids[:, t : t + 1]), coef[:, t : t + 1], 0.0)
    own_row, own_col = iota((8, pn.total), 0), iota((8, pn.total), 1)
    own_at = core * hr + (me // 2) * pn.tok + own_row
    own = jnp.where((own_col == own_at) & (own_row < pn.tok), 1.0, 0.0).astype(BF16)
    own_hidden = mm(own, hidden)

    for k in range(1, ne):
        receive(fr.at[e_of(ne - k)], "f", k - 1, e_dev(k))
    returned = fr[...].reshape(ne * 16, pn.featp).astype(F32)
    mixed = own_hidden + mm(mix, returned, HIGH)
    for r in range(pn.rows):
        out_ref[r] = mixed[r * STEPS : (r + 1) * STEPS, 0 : pn.feat].astype(BF16)
    for copy in pending:
        copy.wait_send()


def on_device(
    nx,
    queries,
    new_latent,
    cache,
    lengths,
    value_up,
    out_proj,
    residual,
    norm_gain,
    route_ids,
    route_weights,
    gate_up,
    expert_down,
):
    ne = lax.axis_size("exp")
    nz = lax.axis_size("ctx") // nx
    pn = Plan(nx, nz, ne, queries, cache, out_proj, gate_up)
    keys = pn.span + LANES
    stat_lanes = nz * pn.block
    any_spec = pl.BlockSpec(memory_space=pl.ANY)
    vmem_spec = pl.BlockSpec(memory_space=pltpu.VMEM)
    smem_spec = pl.BlockSpec(memory_space=pltpu.SMEM)
    fp, total = pn.featp, pn.total
    v = pltpu.VMEM
    scratch = [
        v((pn.rows, STEPS, pn.width, pn.heads), BF16),
        v((pn.rows, pn.width, keys), BF16),
        v(value_up.shape, BF16),
        v(out_proj.shape, BF16),
        v((nx, pn.experts, 2, pn.feat, pn.nzz * pn.fb), BF16),
        v((pn.experts, pn.feat, pn.ffe), BF16),
        v((nx, pn.vrows, nz * fp), BF16),
        v((16, fp), BF16),
        v((ne, 16, fp), BF16),
        v((nx, nz, pn.block, LATENT), BF16),
        v((nx - 1, nz, pn.block, LATENT), BF16),
        v((nx, 8, stat_lanes), F32),
        v((nx - 1, 8, stat_lanes), F32),
        v((nz, pn.block, LATENT), BF16),
        v((nz - 1, pn.block, LATENT), BF16),
        v((8, stat_lanes), F32),
        v((nz - 1, 8, stat_lanes), F32),
        v((stat_lanes, LANES), F32),
        v((stat_lanes, LANES), F32),
        v((pn.hl, pn.block, VDIM), BF16),
        v((ne, pn.block, VDIM), BF16),
        v((nx, 2, total // 2, nz * fp), BF16),
        v((nx, total // 2, nz * fp), BF16),
        v((nx, nz, total // 2, fp), BF16),
        v((nx - 1, nz, total // 2, fp), BF16),
        v((nz, total // 2, fp), BF16),
        v((nz - 1, total // 2, fp), BF16),
        v((total // 2, fp), BF16),
        v((ne, total // 2, fp), BF16),
        v((8, LANES), F32),
        v((nx - 1, 8, LANES), F32),
        v((8, LANES), F32),
        v((nz - 1, 8, LANES), F32),
        v((nx, nz, total, 2 * pn.fb), BF16),
        v((nx - 1, nz, total, 2 * pn.fb), BF16),
        v((nz, total, 2 * pn.fb), BF16),
        v((nz - 1, total, 2 * pn.fb), BF16),
        v((nx, nz, total, pn.fb), BF16),
        v((ne, 16, fp), BF16),
        v((ne, 16, fp), BF16),
        pltpu.SemaphoreType.DMA((pn.n_remote,)),
        pltpu.SemaphoreType.DMA((pn.n_remote,)),
        pltpu.SemaphoreType.DMA((pn.n_local,)),
    ]
    return pl.pallas_call(
        functools.partial(kernel, pn),
        out_shape=jax.ShapeDtypeStruct(residual.shape, BF16),
        in_specs=[
            any_spec,
            vmem_spec,
            any_spec,
            smem_spec,
            any_spec,
            any_spec,
            vmem_spec,
            vmem_spec,
            vmem_spec,
            vmem_spec,
            any_spec,
            any_spec,
        ],
        out_specs=vmem_spec,
        scratch_shapes=scratch,
        compiler_params=pltpu.CompilerParams(
            collective_id=0, has_side_effects=True, vmem_limit_bytes=60 * 1024 * 1024
        ),
        name="decode_layer",
    )(
        jnp.swapaxes(queries, 2, 3),
        new_latent,
        jnp.swapaxes(cache, 1, 2),
        lengths,
        value_up,
        out_proj,
        residual,
        norm_gain,
        route_ids,
        route_weights,
        gate_up,
        jnp.swapaxes(expert_down, 1, 2),
    )


def solution(mesh, nx=CHIPS_X):
    in_specs = (
        P("exp", None, None, None),
        P("exp", None, None),
        P("exp", "ctx", None),
        P("exp"),
        P("ctx", None, None),
        P(("ctx", "exp"), None),
        P("exp", None, "ctx"),
        P("ctx"),
        P("exp", None, None),
        P("exp", None, None),
        P("exp", "ctx", None),
        P("exp", None, "ctx"),
    )
    return jax.shard_map(
        functools.partial(on_device, nx),
        mesh=mesh,
        in_specs=in_specs,
        out_specs=P("exp", None, "ctx"),
        check_vma=False,
    )
```

```python
import functools
import math

import jax
import jax.numpy as jnp
from jax import lax
from jax.experimental import pallas as pl
from jax.experimental.pallas import tpu as pltpu
from jax.sharding import PartitionSpec as P

STEPS = 2
LATENT = 512
VDIM = 128
TOPK = 8
CHIPS_X = 4
LANES = 128

qk_scale = 1.0 / math.sqrt(192.0)
norm_eps = 1e-06
MESH = pl.DeviceIdType.MESH
F32 = jnp.float32
BF16 = jnp.bfloat16
HIGH = lax.Precision.HIGHEST


def iota(shape, dim):
    return lax.broadcasted_iota(jnp.int32, shape, dim)


def log2(n):
    assert n & (n - 1) == 0
    return n.bit_length() - 1


def mm(a, b, precision=None):
    return jnp.dot(a, b, preferred_element_type=F32, precision=precision)


def mm_nt(a, b):
    return lax.dot_general(a, b, (((1,), (1,)), ((), ())), preferred_element_type=F32)


def far_first(n):
    return sorted(range(1, n), key=lambda k: (-min(k, n - k), k))


def pad_lanes(a, width):
    return jnp.concatenate([a, jnp.zeros((a.shape[0], width - a.shape[1]), a.dtype)], axis=1)


def pad_rows(a, height):
    return jnp.concatenate([a, jnp.zeros((height - a.shape[0], a.shape[1]), a.dtype)], axis=0)


class Plan:
    def __init__(self, nx, nz, ne, queries, cache, out_proj, gate_up):
        self.nx, self.nz, self.ne, self.ny = nx, nz, ne, ne // 2
        self.rows = queries.shape[0]
        self.heads = queries.shape[2]
        self.width = queries.shape[3]
        self.span = cache.shape[1]
        self.hl = self.heads // (nx * nz)
        assert self.hl == self.ny
        self.tok = self.rows * STEPS
        self.block = self.tok * self.hl
        self.total = self.tok * ne
        self.model = out_proj.shape[1]
        self.feat = self.model // (nx * nz)
        self.featp = -(-self.feat // LANES) * LANES
        self.vrows = out_proj.shape[0]
        self.ffe = gate_up.shape[2] // 2
        self.experts = gate_up.shape[0]
        self.nzz = nz // self.experts
        self.fb = self.ffe // (nx * self.nzz)
        self.zorder = far_first(nz) + [0]
        self.xorder = far_first(nx) + [0]
        self.halves = 2
        self.per = nz // self.halves
        nxy = nx * self.ny - 1
        self.base, at = {}, 0
        for name, n in (
            ("res", ne - 1),
            ("op", 1),
            ("as", nxy),
            ("a", nxy * self.halves),
            ("azs", nz - 1),
            ("az", nz - 1),
            ("cx", (nx - 1) * self.halves),
            ("cz", nz - 1),
            ("ce", ne - 1),
            ("sx", nx - 1),
            ("sz", nz - 1),
            ("ex", (nx - 1) * self.halves),
            ("ez", nz - 1),
            ("gz", nz - 1),
            ("gx", (nx - 1) * nz),
            ("f", ne - 1),
        ):
            self.base[name] = at
            at += n
        self.n_remote = at
        self.n_local = 2 * self.rows + 10


def joined(tops, totals):
    top = functools.reduce(jnp.maximum, tops)
    raw = [d * jnp.exp(p - top) for p, d in zip(tops, totals)]
    total = functools.reduce(jnp.add, raw)
    inv = jnp.where(total > 0.0, 1.0 / jnp.where(total > 0.0, total, 1.0), 0.0)
    return [r * inv for r in raw], top, total


def kernel(
    pn,
    q_hbm,
    nl_hbm,
    cache_hbm,
    len_hbm,
    vu_hbm,
    op_hbm,
    res_hbm,
    gain_ref,
    ids_hbm,
    rw_hbm,
    gu_hbm,
    dn_hbm,
    out_ref,
    nl_ref,
    len_ref,
    res_ref,
    ids_ref,
    rw_ref,
    qs,
    ks,
    vus,
    ops,
    gus,
    dns,
    opw,
    rb,
    ra,
    os_,
    oxr,
    sxs,
    sxr,
    ozs,
    ozr,
    szs,
    szr,
    xy_cols,
    cs,
    cr,
    zs,
    zr,
    ys,
    yr,
    qxs,
    qxr,
    qzs,
    qzr,
    es,
    exr,
    ezs,
    ezr,
    act,
    fs,
    fr,
    send_sems,
    recv_sems,
    local_sems,
):
    nx, ny, nz, ne = pn.nx, pn.ny, pn.nz, pn.ne
    halves, per = pn.halves, pn.per
    zorder, xorder = pn.zorder, pn.xorder
    ctx = lax.axis_index("ctx")
    me = lax.axis_index("exp")
    my_z, my_x = ctx // nx, lax.rem(ctx, nx)
    my_y, core = me // 2, lax.rem(me, 2)
    pending = []

    def x_of(k):
        return lax.rem(my_x + k, nx)

    def y_of(k):
        return lax.rem(my_y + k, ny)

    def z_of(k):
        return lax.rem(my_z + k, nz)

    def e_of(k):
        return lax.rem(me + k, ne)

    def x_dev(k):
        return (my_z * nx + x_of(k), me)

    def xy_dev(kx, ky):
        return (my_z * nx + x_of(kx), 2 * y_of(ky) + core)

    def z_dev(k):
        return (z_of(k) * nx + my_x, me)

    def e_dev(k):
        return (ctx, e_of(k))

    core_dev = (ctx, me + 1 - 2 * core)

    xy_far = [
        (kx, ky) for kx in far_first(nx) + [0] for ky in far_first(ny) + [0] if kx or ky
    ]
    barrier = pltpu.get_barrier_semaphore()
    peers = (
        [z_dev(k) for k in far_first(nz)]
        + [xy_dev(kx, ky) for kx, ky in xy_far]
        + [(ctx, 2 * y_of(ky) + 1 - core) for ky in range(ny)]
    )
    for dev in peers:
        pl.semaphore_signal(barrier, inc=1, device_id=dev, device_id_type=MESH)

    def remote(src, dst, name, slot, dev):
        at = pn.base[name] + slot
        return pltpu.make_async_remote_copy(
            src_ref=src,
            dst_ref=dst,
            send_sem=send_sems.at[at],
            recv_sem=recv_sems.at[at],
            device_id=dev,
            device_id_type=MESH,
        )

    def send(src, dst, name, slot, dev):
        copy = remote(src, dst, name, slot, dev)
        copy.start()
        pending.append(copy)

    def receive(dst, name, slot, dev):
        remote(dst, dst, name, slot, dev).wait_recv()

    local_at = [0]

    def local(src, dst):
        copy = pltpu.make_async_copy(src, dst, local_sems.at[local_at[0]])
        local_at[0] += 1
        copy.start()
        return copy

    q_copies = [local(q_hbm.at[r], qs.at[r]) for r in range(pn.rows)]
    k_copies = [
        local(cache_hbm.at[r], ks.at[r, :, pl.ds(0, pn.span)]) for r in range(pn.rows)
    ]
    small_copies = [
        local(nl_hbm, nl_ref),
        local(len_hbm, len_ref),
        local(res_hbm, res_ref),
        local(ids_hbm, ids_ref),
        local(rw_hbm, rw_ref),
    ]
    op_copy = local(op_hbm, ops.at[core])
    vu_copy = local(vu_hbm.at[my_y], vus)

    qrows = STEPS * pn.heads
    keys = pn.span + LANES
    lp, lh, lhl = log2(per), log2(halves), log2(pn.hl)
    m = iota((qrows, qrows), 0)
    m_place = (m >> 1) & (nz - 1)
    m_head = (m >> (1 + lp + lh)) & (pn.hl - 1)
    m_x = m >> (1 + lp + lh + lhl)
    m_z = jnp.zeros_like(m)
    for place, k in enumerate(zorder):
        m_z = jnp.where(m_place == place, z_of(k), m_z)
    source = (m & (STEPS - 1)) * pn.heads + (m_z * nx + m_x) * pn.hl + m_head
    perm = jnp.where(iota((qrows, qrows), 1) == source, 1.0, 0.0).astype(BF16)

    col = iota((qrows, keys), 1)
    step = iota((qrows, keys), 0) & (STEPS - 1)
    first = jnp.where(ctx == 0, 0, -LANES)
    is_fresh = (col >= pn.span) & (col - pn.span <= step + first)
    position = ctx * pn.span + col

    for copy in small_copies:
        copy.wait()
    for r in range(pn.rows):
        fresh = pad_lanes(nl_ref[r].astype(F32), -(-pn.width // LANES) * LANES)
        fresh = jnp.transpose(pad_rows(fresh, LANES))[0 : pn.width, :]
        ks[r, :, pl.ds(pn.span, LANES)] = fresh.astype(BF16)
    res_rows = jnp.concatenate([res_ref[r].astype(F32) for r in range(pn.rows)], axis=0)
    rb[...] = pad_rows(pad_lanes(res_rows, pn.featp), 16).astype(BF16)
    ra[me] = rb[...]

    gu_sem, dn_copy = local_sems.at[pn.n_local - 1], None
    partial, peaks, denoms = [], [], []
    for r in range(pn.rows):
        q_copies[r].wait()
        k_copies[r].wait()
        if r == pn.rows - 1:
            for x in range(nx):
                for z in range(nz):
                    j, zz = z // pn.nzz, z % pn.nzz
                    for g in range(2):
                        at = g * pn.ffe + (x * pn.nzz + zz) * pn.fb
                        pltpu.make_async_copy(
                            gu_hbm.at[j, :, pl.ds(at, pn.fb)],
                            gus.at[x, z, :, pl.ds(g * pn.fb, pn.fb)],
                            gu_sem,
                        ).start()
            dn_copy = local(dn_hbm, dns)
        qp = functools.reduce(
            jnp.add,
            [
                mm_nt(perm[:, s * pn.heads : (s + 1) * pn.heads], qs[r, s])
                for s in range(STEPS)
            ],
        ).astype(BF16)
        scores = mm(qp, ks[r])
        visible = ((col < pn.span) & (position < len_ref[r])) | is_fresh
        scores = jnp.where(visible, scores * qk_scale, -1e30)
        peak = jnp.max(scores, axis=1, keepdims=True)
        weights = jnp.where(visible, jnp.exp(scores - peak), 0.0)
        denom = jnp.sum(weights, axis=1, keepdims=True)
        mixture = mm_nt(weights.astype(BF16), ks[r, pl.ds(0, LATENT), :])
        inv = jnp.where(denom > 0.0, 1.0 / jnp.where(denom > 0.0, denom, 1.0), 0.0)
        partial.append(mixture * inv)
        peaks.append(peak)
        denoms.append(denom)

    span_rows = STEPS * per
    groups = nx * pn.hl * halves
    lane = iota((qrows, LANES), 1)
    stat = [
        jnp.where(lane == 0, p, jnp.where(lane == 1, d, 0.0)) for p, d in zip(peaks, denoms)
    ]
    stat = jnp.concatenate([s.reshape(groups, span_rows, LANES) for s in stat], axis=1)
    stat = stat.reshape(nx, nz * pn.block, LANES)
    for x in range(nx):
        sxs[x] = jnp.transpose(stat[x])[0:8, :]
    sxr[0, my_y] = sxs[my_x]
    crow = pn.rows * span_rows
    merged = jnp.concatenate(
        [p.reshape(groups, span_rows, LATENT) for p in partial], axis=1
    )
    os_[...] = merged.astype(BF16).reshape(nx, pn.hl, halves, crow, LATENT)
    oxr[0, my_y] = os_[my_x, my_y]

    pl.semaphore_wait(barrier, len(peers))
    for kx, ky in xy_far:
        slot = kx * ny + ky - 1
        send(sxs.at[x_of(kx)], sxr.at[kx, my_y], "as", slot, xy_dev(kx, ky))
    for h in range(halves):
        for kx, ky in xy_far:
            slot = (kx * ny + ky - 1) * halves + h
            send(
                os_.at[x_of(kx), y_of(ky), h],
                oxr.at[kx, my_y, h],
                "a",
                slot,
                xy_dev(kx, ky),
            )
    op_copy.wait()
    send(ops.at[core], ops.at[core], "op", 0, core_dev)
    for k in range(1, ne):
        send(rb, ra.at[me], "res", k - 1, e_dev(k))

    for kx, ky in reversed(xy_far):
        src_y = y_of(ny - ky)
        receive(sxr.at[kx, src_y], "as", kx * ny + ky - 1, xy_dev(kx, ky))
    tops = [
        jnp.concatenate([sxr[kx, y, 0:1, :] for y in range(ny)], axis=0) for kx in range(nx)
    ]
    totals = [
        jnp.concatenate([sxr[kx, y, 1:2, :] for y in range(ny)], axis=0) for kx in range(nx)
    ]
    coefs, top, total = joined(tops, totals)
    table = pad_rows(jnp.concatenate(coefs + [top, total], axis=0), LANES)
    xy_cols[...] = jnp.transpose(table)
    mine = halves * crow
    cols = xy_cols[pl.ds(pl.multiple_of(my_y * mine, mine), mine), :]

    hrows = ny * crow
    lrow, ly = log2(pn.rows), log2(ny)
    a = iota((hrows, hrows), 0)
    a_step, a_row = a & 1, (a >> 1) & (pn.rows - 1)
    a_y, a_place = (a >> (1 + lrow)) & (ny - 1), a >> (1 + lrow + ly)
    a_from = a_y * crow + a_row * span_rows + a_place * STEPS + a_step
    turn = jnp.where(iota((hrows, hrows), 1) == a_from, 1.0, 0.0)
    lane = iota((crow, LANES), 1)
    stat = []
    for h in range(halves):
        at = slice(h * crow, (h + 1) * crow)
        rows = [
            jnp.where(
                lane == 0,
                cols[at, nx * ny + y : nx * ny + y + 1],
                jnp.where(lane == 1, cols[at, (nx + 1) * ny + y : (nx + 1) * ny + y + 1], 0.0),
            )
            for y in range(ny)
        ]
        stat.append(mm(turn, jnp.concatenate(rows, axis=0), HIGH))
    szs[...] = jnp.transpose(jnp.concatenate(stat, axis=0))[0:8, :]
    for k in far_first(nz):
        send(szs, szr.at[k - 1], "azs", k - 1, z_dev(k))
    turn = turn.astype(BF16)
    for h in range(halves):
        for kx, ky in reversed(xy_far):
            slot = (kx * ny + ky - 1) * halves + h
            receive(oxr.at[kx, y_of(ny - ky), h], "a", slot, xy_dev(kx, ky))
        at = slice(h * crow, (h + 1) * crow)
        sums = []
        for y in range(ny):
            acc = cols[at, y : y + 1] * oxr[0, y, h].astype(F32)
            for kx in range(1, nx):
                c = kx * ny + y
                acc = acc + cols[at, c : c + 1] * oxr[kx, y, h].astype(F32)
            sums.append(acc.astype(BF16))
        turned = mm(turn, jnp.concatenate(sums, axis=0)).astype(BF16)
        for p in range(per):
            place = h * per + p
            ozs[place] = turned[p * pn.block : (p + 1) * pn.block, :]
            k = zorder[place]
            if k > 0:
                send(ozs.at[place], ozr.at[k - 1], "az", k - 1, z_dev(k))

    receive(ops.at[1 - core], "op", 0, core_dev)
    for z in range(nz):
        for x in range(nx):
            c = z * nx + x
            for half in range(2):
                piece = ops[half, :, c * pn.feat : (c + 1) * pn.feat]
                opw[x, z, half * pn.vrows : (half + 1) * pn.vrows, :] = pad_lanes(
                    piece, pn.featp
                )
    for k in range(1, ne):
        receive(ra.at[e_of(ne - k)], "res", k - 1, e_dev(k))
    lt = log2(pn.tok)

    def owner_of(n):
        y = (n >> lt) & (ny - 1)
        return 2 * y + (n >> (lt + ly)), n & (pn.tok - 1)

    n_row = iota((pn.total, ne * 16), 0)
    n_owner, n_tok = owner_of(n_row)
    spread = iota((pn.total, ne * 16), 1)
    pick = jnp.where(spread == n_owner * 16 + n_tok, 1.0, 0.0).astype(BF16)
    residual = mm(pick, ra[...].reshape(ne * 16, pn.featp))
    vu_copy.wait()

    def stat_of(ref, k):
        at = zorder.index(k) * pn.block
        return pad_lanes(ref[0:2, at : at + pn.block], LANES)

    for k in range(1, nz):
        receive(szr.at[k - 1], "azs", k - 1, z_dev(k))
    stat = [stat_of(szs, 0)] + [stat_of(szr.at[k - 1], k) for k in range(1, nz)]
    coefs, _, _ = joined([s[0:1, :] for s in stat], [s[1:2, :] for s in stat])
    cols = jnp.transpose(pad_rows(jnp.concatenate(coefs, axis=0), LANES))[0 : pn.block, :]
    acc = cols[:, 0:1] * ozs[nz - 1].astype(F32)
    for k in reversed(far_first(nz)):
        receive(ozr.at[k - 1], "az", k - 1, z_dev(k))
        acc = acc + cols[:, k : k + 1] * ozr[k - 1].astype(F32)
    values = mm(acc.astype(BF16), vus[...]).astype(BF16)

    def partner_chunk(h):
        return pl.ds(h * per, per)

    for h in range(halves):
        for k in xorder:
            for p in range(per):
                place = h * per + p
                block = mm(values, opw[x_of(k), z_of(zorder[place])])
                cs[k, place] = block.astype(BF16)
            if k > 0:
                send(
                    cs.at[k, partner_chunk(h)],
                    cr.at[k - 1, partner_chunk(h)],
                    "cx",
                    (k - 1) * halves + h,
                    x_dev(k),
                )
    for h in range(halves):
        for k in range(1, nx):
            receive(
                cr.at[k - 1, partner_chunk(h)], "cx", (k - 1) * halves + h, x_dev(k)
            )
        for p in range(per):
            place = h * per + p
            acc = cs[0, place].astype(F32)
            for i in range(1, nx):
                acc = acc + cr[i - 1, place].astype(F32)
            zs[place] = acc.astype(BF16)
            k = zorder[place]
            if k > 0:
                send(zs.at[place], zr.at[k - 1], "cz", k - 1, z_dev(k))
    acc = zs[nz - 1].astype(F32)
    for k in reversed(far_first(nz)):
        receive(zr.at[k - 1], "cz", k - 1, z_dev(k))
        acc = acc + zr[k - 1].astype(F32)
    ys[...] = acc.astype(BF16)
    for k in far_first(ne):
        send(ys, yr.at[me], "ce", k - 1, e_dev(k))
    yr[me] = ys[...]
    for k in range(1, ne):
        receive(yr.at[e_of(ne - k)], "ce", k - 1, e_dev(k))
    sides = []
    for c in range(2):
        acc = yr[c].astype(F32)
        for y in range(1, ny):
            acc = acc + yr[2 * y + c].astype(F32)
        sides.append(acc)
    hidden = (residual + jnp.concatenate(sides, axis=0)).astype(BF16)
    hidden_f = hidden.astype(F32)

    scaled = (hidden_f[:, 0 : pn.feat] * gain_ref[...].reshape(1, pn.feat)).astype(BF16)
    pltpu.make_async_copy(gus, gus, gu_sem).wait()
    fb = pn.fb
    for h in range(halves):
        for k in xorder:
            for p in range(per):
                place = h * per + p
                block = mm(scaled, gus[x_of(k), z_of(zorder[place])])
                es[k, place] = block.astype(BF16)
            if k > 0:
                send(
                    es.at[k, partner_chunk(h)],
                    exr.at[k - 1, partner_chunk(h)],
                    "ex",
                    (k - 1) * halves + h,
                    x_dev(k),
                )
        if h == 0:
            squares = jnp.sum(hidden_f * hidden_f, axis=1, keepdims=True)
            squares = pad_rows(jnp.broadcast_to(squares, (pn.total, LANES)), LANES)
            qxs[...] = jnp.transpose(squares)[0:8, :]
            for k in far_first(nx):
                send(qxs, qxr.at[k - 1], "sx", k - 1, x_dev(k))
    acc = qxs[...]
    for k in range(1, nx):
        receive(qxr.at[k - 1], "sx", k - 1, x_dev(k))
        acc = acc + qxr[k - 1]
    qzs[...] = acc
    for h in range(halves):
        for k in range(1, nx):
            receive(
                exr.at[k - 1, partner_chunk(h)], "ex", (k - 1) * halves + h, x_dev(k)
            )
        for p in range(per):
            place = h * per + p
            acc = es[0, place].astype(F32)
            for i in range(1, nx):
                acc = acc + exr[i - 1, place].astype(F32)
            ezs[place] = acc.astype(BF16)
            k = zorder[place]
            if k > 0:
                send(ezs.at[place], ezr.at[k - 1], "ez", k - 1, z_dev(k))
                send(qzs, qzr.at[k - 1], "sz", k - 1, z_dev(k))
    acc = qzs[...]
    for k in range(1, nz):
        receive(qzr.at[k - 1], "sz", k - 1, z_dev(k))
        acc = acc + qzr[k - 1]
    scale_row = lax.rsqrt(acc / pn.model + norm_eps)
    scale = jnp.transpose(pad_rows(scale_row, LANES))[0 : pn.total, 0:1]
    acc = ezs[nz - 1].astype(F32)
    for k in reversed(far_first(nz)):
        receive(ezr.at[k - 1], "ez", k - 1, z_dev(k))
        acc = acc + ezr[k - 1].astype(F32)
    acc = acc * scale
    gate, up = acc[:, 0:fb], acc[:, fb : 2 * fb]
    activated = gate / (1.0 + jnp.exp(-gate)) * up
    act[my_x, my_z] = activated.astype(BF16)

    for k in far_first(nz):
        send(act.at[my_x, my_z], act.at[my_x, my_z], "gz", k - 1, z_dev(k))
    dn_copy.wait()
    for k in [0] + list(reversed(far_first(nz))):
        block = act.at[my_x, z_of(nz - k)]
        if k > 0:
            receive(block, "gz", k - 1, z_dev(k))
        for i in far_first(nx):
            send(block, block, "gx", (i - 1) * nz + k, x_dev(i))
    depth = pn.nzz * fb
    outs = [jnp.zeros((pn.total, pn.feat), F32) for _ in range(pn.experts)]
    for k in range(nx):
        xp = x_of(nx - k)
        if k > 0:
            for i in range(nz):
                receive(act.at[xp, z_of(nz - i)], "gx", (k - 1) * nz + i, x_dev(k))
        for j in range(pn.experts):
            rows = jnp.concatenate(
                [act[xp, j * pn.nzz + zz] for zz in range(pn.nzz)], axis=1
            )
            down = dns[j, :, pl.ds(pl.multiple_of(xp * depth, depth), depth)]
            outs[j] = outs[j] + mm_nt(rows, down)

    s_row = iota((ne * 16, pn.total), 0)
    s_owner, s_tok = owner_of(iota((ne * 16, pn.total), 1))
    acc = jnp.zeros((ne * 16, pn.featp), F32)
    for j in range(pn.experts):
        put = jnp.where(s_row == s_owner * 16 + j * pn.tok + s_tok, 1.0, 0.0).astype(BF16)
        acc = acc + mm(put, pad_lanes(outs[j], pn.featp).astype(BF16))
    fs[...] = acc.astype(BF16).reshape(ne, 16, pn.featp)
    for k in far_first(ne):
        send(fs.at[e_of(k)], fr.at[me], "f", k - 1, e_dev(k))
    fr[me] = fs[me]

    ids = pad_rows(jnp.concatenate([ids_ref[r] for r in range(pn.rows)], axis=0), 8)
    coef = pad_rows(jnp.concatenate([rw_ref[r] for r in range(pn.rows)], axis=0), 8)
    c_row, c_col = iota((8, ne * 16), 0), iota((8, ne * 16), 1)
    place = c_col & 15
    expert = (c_col >> 4) * pn.experts + (place >> lt)
    used = (place < pn.experts * pn.tok) & ((place & (pn.tok - 1)) == c_row)
    mix = jnp.zeros((8, ne * 16), F32)
    for t in range(TOPK):
        mix = mix + jnp.where(used & (expert == ids[:, t : t + 1]), coef[:, t : t + 1], 0.0)
    own_row, own_col = iota((8, pn.total), 0), iota((8, pn.total), 1)
    own_at = core * (pn.total // 2) + my_y * pn.tok + own_row
    own = jnp.where((own_col == own_at) & (own_row < pn.tok), 1.0, 0.0).astype(BF16)
    own_hidden = mm(own, hidden)

    for k in range(1, ne):
        receive(fr.at[e_of(ne - k)], "f", k - 1, e_dev(k))
    returned = fr[...].reshape(ne * 16, pn.featp).astype(F32)
    mixed = own_hidden + mm(mix, returned, HIGH)
    for r in range(pn.rows):
        out_ref[r] = mixed[r * STEPS : (r + 1) * STEPS, 0 : pn.feat].astype(BF16)
    for copy in pending:
        copy.wait_send()


def on_device(
    nx,
    queries,
    new_latent,
    cache,
    lengths,
    value_up,
    out_proj,
    residual,
    norm_gain,
    route_ids,
    route_weights,
    gate_up,
    expert_down,
):
    ne = lax.axis_size("exp")
    nz = lax.axis_size("ctx") // nx
    pn = Plan(nx, nz, ne, queries, cache, out_proj, gate_up)
    keys = pn.span + LANES
    stat_lanes = nz * pn.block
    any_spec = pl.BlockSpec(memory_space=pl.ANY)
    vmem_spec = pl.BlockSpec(memory_space=pltpu.VMEM)
    fp, total = pn.featp, pn.total
    v = pltpu.VMEM
    crow = pn.rows * STEPS * pn.per
    scratch = [
        v(new_latent.shape, BF16),
        pltpu.SMEM(lengths.shape, jnp.int32),
        v(residual.shape, BF16),
        v(route_ids.shape, jnp.int32),
        v(route_weights.shape, F32),
        v((pn.rows, STEPS, pn.width, pn.heads), BF16),
        v((pn.rows, pn.width, keys), BF16),
        v(value_up.shape[1:], BF16),
        v((2, *out_proj.shape), BF16),
        v((nx, nz, pn.feat, 2 * pn.fb), BF16),
        v((pn.experts, pn.feat, pn.ffe), BF16),
        v((nx, nz, 2 * pn.vrows, fp), BF16),
        v((16, fp), BF16),
        v((ne, 16, fp), BF16),
        v((nx, pn.hl, pn.halves, crow, LATENT), BF16),
        v((nx, pn.ny, pn.halves, crow, LATENT), BF16),
        v((nx, 8, stat_lanes), F32),
        v((nx, pn.ny, 8, stat_lanes), F32),
        v((nz, pn.block, LATENT), BF16),
        v((nz - 1, pn.block, LATENT), BF16),
        v((8, stat_lanes), F32),
        v((nz - 1, 8, stat_lanes), F32),
        v((stat_lanes, LANES), F32),
        v((nx, nz, total // 2, fp), BF16),
        v((nx - 1, nz, total // 2, fp), BF16),
        v((nz, total // 2, fp), BF16),
        v((nz - 1, total // 2, fp), BF16),
        v((total // 2, fp), BF16),
        v((ne, total // 2, fp), BF16),
        v((8, LANES), F32),
        v((nx - 1, 8, LANES), F32),
        v((8, LANES), F32),
        v((nz - 1, 8, LANES), F32),
        v((nx, nz, total, 2 * pn.fb), BF16),
        v((nx - 1, nz, total, 2 * pn.fb), BF16),
        v((nz, total, 2 * pn.fb), BF16),
        v((nz - 1, total, 2 * pn.fb), BF16),
        v((nx, nz, total, pn.fb), BF16),
        v((ne, 16, fp), BF16),
        v((ne, 16, fp), BF16),
        pltpu.SemaphoreType.DMA((pn.n_remote,)),
        pltpu.SemaphoreType.DMA((pn.n_remote,)),
        pltpu.SemaphoreType.DMA((pn.n_local,)),
    ]
    return pl.pallas_call(
        functools.partial(kernel, pn),
        out_shape=jax.ShapeDtypeStruct(residual.shape, BF16),
        in_specs=[any_spec] * 7 + [vmem_spec] + [any_spec] * 4,
        out_specs=vmem_spec,
        scratch_shapes=scratch,
        compiler_params=pltpu.CompilerParams(
            collective_id=0, has_side_effects=True, vmem_limit_bytes=60 * 1024 * 1024
        ),
        name="decode_layer",
    )(
        jnp.swapaxes(queries, 2, 3),
        new_latent,
        jnp.swapaxes(cache, 1, 2),
        lengths,
        value_up,
        out_proj,
        residual,
        norm_gain,
        route_ids,
        route_weights,
        gate_up,
        jnp.swapaxes(expert_down, 1, 2),
    )


def solution(mesh, nx=CHIPS_X):
    in_specs = (
        P("exp", None, None, None),
        P("exp", None, None),
        P("exp", "ctx", None),
        P("exp"),
        P("ctx", None, None),
        P(("ctx", "exp"), None),
        P("exp", None, "ctx"),
        P("ctx"),
        P("exp", None, None),
        P("exp", None, None),
        P("exp", "ctx", None),
        P("exp", None, "ctx"),
    )
    return jax.shard_map(
        functools.partial(on_device, nx),
        mesh=mesh,
        in_specs=in_specs,
        out_specs=P("exp", None, "ctx"),
        check_vma=False,
    )
```

```python
import functools
import math

import jax
import jax.numpy as jnp
from jax import lax
from jax.experimental import pallas as pl
from jax.experimental.pallas import tpu as pltpu
from jax.sharding import PartitionSpec as P

STEPS = 2
LATENT = 512
VDIM = 128
TOPK = 8
CHIPS_X = 4
LANES = 128

qk_scale = 1.0 / math.sqrt(192.0)
norm_eps = 1e-06
MESH = pl.DeviceIdType.MESH
F32 = jnp.float32
BF16 = jnp.bfloat16
HIGH = lax.Precision.HIGHEST


def iota(shape, dim):
    return lax.broadcasted_iota(jnp.int32, shape, dim)


def log2(n):
    assert n & (n - 1) == 0
    return n.bit_length() - 1


def mm(a, b, precision=None):
    return jnp.dot(a, b, preferred_element_type=F32, precision=precision)


def mm_nt(a, b):
    return lax.dot_general(a, b, (((1,), (1,)), ((), ())), preferred_element_type=F32)


def far_first(n):
    return sorted(range(1, n), key=lambda k: (-min(k, n - k), k))


def pad_lanes(a, width):
    return jnp.concatenate([a, jnp.zeros((a.shape[0], width - a.shape[1]), a.dtype)], axis=1)


def pad_rows(a, height):
    return jnp.concatenate([a, jnp.zeros((height - a.shape[0], a.shape[1]), a.dtype)], axis=0)


class Plan:
    def __init__(self, nx, nz, ne, queries, cache, out_proj, gate_up):
        self.nx, self.nz, self.ne, self.ny = nx, nz, ne, ne // 2
        self.rows = queries.shape[0]
        self.heads = queries.shape[2]
        self.width = queries.shape[3]
        self.span = cache.shape[1]
        self.hl = self.heads // (nx * nz)
        assert self.hl == self.ny
        self.tok = self.rows * STEPS
        self.block = self.tok * self.hl
        self.total = self.tok * ne
        self.model = out_proj.shape[1]
        self.feat = self.model // (nx * nz)
        self.featp = -(-self.feat // LANES) * LANES
        self.vrows = out_proj.shape[0]
        self.ffe = gate_up.shape[2] // 2
        self.experts = gate_up.shape[0]
        self.nzz = nz // self.experts
        self.fb = self.ffe // (nx * self.nzz)
        self.zorder = far_first(nz) + [0]
        self.xorder = far_first(nx) + [0]
        self.halves = 2
        self.parts = min(4, nz)
        self.per = nz // self.halves
        nxy = nx * self.ny - 1
        self.base, at = {}, 0
        for name, n in (
            ("res", ne - 1),
            ("op", 1),
            ("as", nxy),
            ("a", nxy * self.halves),
            ("azs", nz - 1),
            ("az", nz - 1),
            ("cx", (nx - 1) * self.parts),
            ("cz", nz - 1),
            ("ce", ne - 1),
            ("sx", nx - 1),
            ("sz", nz - 1),
            ("ex", (nx - 1) * self.parts),
            ("ez", nz - 1),
            ("gz", nz - 1),
            ("gx", (nx - 1) * nz),
            ("f", ne - 1),
        ):
            self.base[name] = at
            at += n
        self.n_remote = at
        self.n_local = 2 * self.rows + 12


def joined(tops, totals):
    top = functools.reduce(jnp.maximum, tops)
    raw = [d * jnp.exp(p - top) for p, d in zip(tops, totals)]
    total = functools.reduce(jnp.add, raw)
    inv = jnp.where(total > 0.0, 1.0 / jnp.where(total > 0.0, total, 1.0), 0.0)
    return [r * inv for r in raw], top, total


def kernel(
    pn,
    q_hbm,
    nl_hbm,
    cache_hbm,
    len_hbm,
    vu_hbm,
    op_hbm,
    res_hbm,
    gain_hbm,
    ids_hbm,
    rw_hbm,
    gu_hbm,
    dn_hbm,
    out_ref,
    nl_ref,
    len_ref,
    res_ref,
    gain_ref,
    ids_ref,
    rw_ref,
    qs,
    ks,
    vus,
    ops,
    gus,
    dns,
    opw,
    rb,
    ra,
    os_,
    oxr,
    sxs,
    sxr,
    ozs,
    ozr,
    szs,
    szr,
    xy_cols,
    cs,
    cr,
    zs,
    zr,
    ys,
    yr,
    qxs,
    qxr,
    qzs,
    qzr,
    es,
    exr,
    ezs,
    ezr,
    act,
    fs,
    fr,
    send_sems,
    recv_sems,
    local_sems,
):
    nx, ny, nz, ne = pn.nx, pn.ny, pn.nz, pn.ne
    halves, per = pn.halves, pn.per
    zorder, xorder = pn.zorder, pn.xorder
    ctx = lax.axis_index("ctx")
    me = lax.axis_index("exp")
    my_z, my_x = ctx // nx, lax.rem(ctx, nx)
    my_y, core = me // 2, lax.rem(me, 2)
    pending = []

    def x_of(k):
        return lax.rem(my_x + k, nx)

    def y_of(k):
        return lax.rem(my_y + k, ny)

    def z_of(k):
        return lax.rem(my_z + k, nz)

    def e_of(k):
        return lax.rem(me + k, ne)

    def x_dev(k):
        return (my_z * nx + x_of(k), me)

    def xy_dev(kx, ky):
        return (my_z * nx + x_of(kx), 2 * y_of(ky) + core)

    def z_dev(k):
        return (z_of(k) * nx + my_x, me)

    def e_dev(k):
        return (ctx, e_of(k))

    core_dev = (ctx, me + 1 - 2 * core)

    local_at = [0]

    def local(src, dst):
        copy = pltpu.make_async_copy(src, dst, local_sems.at[local_at[0]])
        local_at[0] += 1
        copy.start()
        return copy

    q_copies, k_copies = [], []
    for r in range(pn.rows):
        q_copies.append(local(q_hbm.at[r], qs.at[r]))
        k_copies.append(local(cache_hbm.at[r], ks.at[r, :, pl.ds(0, pn.span)]))
    small_copies = [
        local(nl_hbm, nl_ref),
        local(len_hbm, len_ref),
        local(res_hbm, res_ref),
        local(ids_hbm, ids_ref),
        local(rw_hbm, rw_ref),
        local(gain_hbm, gain_ref),
    ]

    xy_far = [
        (kx, ky) for kx in far_first(nx) + [0] for ky in far_first(ny) + [0] if kx or ky
    ]
    barrier = pltpu.get_barrier_semaphore()
    peers = (
        [z_dev(k) for k in far_first(nz)]
        + [xy_dev(kx, ky) for kx, ky in xy_far]
        + [(ctx, 2 * y_of(ky) + 1 - core) for ky in range(ny)]
    )
    for dev in peers:
        pl.semaphore_signal(barrier, inc=1, device_id=dev, device_id_type=MESH)

    def remote(src, dst, name, slot, dev):
        at = pn.base[name] + slot
        return pltpu.make_async_remote_copy(
            src_ref=src,
            dst_ref=dst,
            send_sem=send_sems.at[at],
            recv_sem=recv_sems.at[at],
            device_id=dev,
            device_id_type=MESH,
        )

    def send(src, dst, name, slot, dev):
        copy = remote(src, dst, name, slot, dev)
        copy.start()
        pending.append(copy)

    def receive(dst, name, slot, dev):
        remote(dst, dst, name, slot, dev).wait_recv()

    qrows = STEPS * pn.heads
    keys = pn.span + LANES
    lp, lh, lhl = log2(per), log2(halves), log2(pn.hl)
    m = iota((qrows, qrows), 0)
    m_place = (m >> 1) & (nz - 1)
    m_head = (m >> (1 + lp + lh)) & (pn.hl - 1)
    m_x = m >> (1 + lp + lh + lhl)
    m_z = jnp.zeros_like(m)
    for place, k in enumerate(zorder):
        m_z = jnp.where(m_place == place, z_of(k), m_z)
    source = (m & (STEPS - 1)) * pn.heads + (m_z * nx + m_x) * pn.hl + m_head
    perm = jnp.where(iota((qrows, qrows), 1) == source, 1.0, 0.0).astype(BF16)

    col = iota((qrows, keys), 1)
    step = iota((qrows, keys), 0) & (STEPS - 1)
    first = jnp.where(ctx == 0, 0, -LANES)
    is_fresh = (col >= pn.span) & (col - pn.span <= step + first)
    position = ctx * pn.span + col

    for copy in small_copies:
        copy.wait()
    for r in range(pn.rows):
        fresh = pad_lanes(nl_ref[r].astype(F32), -(-pn.width // LANES) * LANES)
        fresh = jnp.transpose(pad_rows(fresh, LANES))[0 : pn.width, :]
        ks[r, :, pl.ds(pn.span, LANES)] = fresh.astype(BF16)
    res_rows = jnp.concatenate([res_ref[r].astype(F32) for r in range(pn.rows)], axis=0)
    rb[...] = pad_rows(pad_lanes(res_rows, pn.featp), 16).astype(BF16)
    ra[me] = rb[...]

    partial, peaks, denoms = [], [], []
    for r in range(pn.rows):
        q_copies[r].wait()
        k_copies[r].wait()
        qp = functools.reduce(
            jnp.add,
            [
                mm_nt(perm[:, s * pn.heads : (s + 1) * pn.heads], qs[r, s])
                for s in range(STEPS)
            ],
        ).astype(BF16)
        scores = mm(qp, ks[r])
        visible = ((col < pn.span) & (position < len_ref[r])) | is_fresh
        scores = jnp.where(visible, scores * qk_scale, -1e30)
        peak = jnp.max(scores, axis=1, keepdims=True)
        weights = jnp.where(visible, jnp.exp(scores - peak), 0.0)
        denom = jnp.sum(weights, axis=1, keepdims=True)
        mixture = mm_nt(weights.astype(BF16), ks[r, pl.ds(0, LATENT), :])
        inv = jnp.where(denom > 0.0, 1.0 / jnp.where(denom > 0.0, denom, 1.0), 0.0)
        partial.append(mixture * inv)
        peaks.append(peak)
        denoms.append(denom)

    span_rows = STEPS * per
    groups = nx * pn.hl * halves
    crow = pn.rows * span_rows
    merged = jnp.concatenate(
        [p.reshape(groups, span_rows, LATENT) for p in partial], axis=1
    )
    os_[...] = merged.astype(BF16).reshape(nx, pn.hl, halves, crow, LATENT)

    def send_partial(h):
        for kx, ky in xy_far:
            send(
                os_.at[x_of(kx), y_of(ky), h],
                oxr.at[kx, my_y, h],
                "a",
                (kx * ny + ky - 1) * halves + h,
                xy_dev(kx, ky),
            )

    pl.semaphore_wait(barrier, len(peers))
    send_partial(0)
    lane = iota((qrows, LANES), 1)
    stat = [
        jnp.where(lane == 0, p, jnp.where(lane == 1, d, 0.0)) for p, d in zip(peaks, denoms)
    ]
    stat = jnp.concatenate([s.reshape(groups, span_rows, LANES) for s in stat], axis=1)
    stat = stat.reshape(nx, nz * pn.block, LANES)
    for x in range(nx):
        sxs[x] = jnp.transpose(stat[x])[0:2, :]
    for kx, ky in xy_far:
        slot = kx * ny + ky - 1
        send(sxs.at[x_of(kx)], sxr.at[kx, my_y], "as", slot, xy_dev(kx, ky))
    for h in range(1, halves):
        send_partial(h)
    sxr[0, my_y] = sxs[my_x]
    oxr[0, my_y] = os_[my_x, my_y]
    op_copy = local(op_hbm, ops.at[core])
    vu_copy = local(vu_hbm.at[my_y], vus)
    gu_sem = local_sems.at[pn.n_local - 1]
    for x in range(nx):
        for z in range(nz):
            j, zz = z // pn.nzz, z % pn.nzz
            for g in range(2):
                at = g * pn.ffe + (x * pn.nzz + zz) * pn.fb
                pltpu.make_async_copy(
                    gu_hbm.at[j, :, pl.ds(at, pn.fb)],
                    gus.at[x, z, :, pl.ds(g * pn.fb, pn.fb)],
                    gu_sem,
                ).start()
    dn_copy = local(dn_hbm, dns)
    op_copy.wait()
    send(ops.at[core], ops.at[core], "op", 0, core_dev)
    for k in range(1, ne):
        send(rb, ra.at[me], "res", k - 1, e_dev(k))

    for kx, ky in reversed(xy_far):
        src_y = y_of(ny - ky)
        receive(sxr.at[kx, src_y], "as", kx * ny + ky - 1, xy_dev(kx, ky))
    tops = [
        jnp.concatenate([sxr[kx, y, 0:1, :] for y in range(ny)], axis=0) for kx in range(nx)
    ]
    totals = [
        jnp.concatenate([sxr[kx, y, 1:2, :] for y in range(ny)], axis=0) for kx in range(nx)
    ]
    coefs, top, total = joined(tops, totals)
    table = pad_rows(jnp.concatenate(coefs + [top, total], axis=0), LANES)
    xy_cols[...] = jnp.transpose(table)
    mine = halves * crow
    cols = xy_cols[pl.ds(pl.multiple_of(my_y * mine, mine), mine), :]

    hrows = ny * crow
    lrow, ly = log2(pn.rows), log2(ny)
    a = iota((hrows, hrows), 0)
    a_step, a_row = a & 1, (a >> 1) & (pn.rows - 1)
    a_y, a_place = (a >> (1 + lrow)) & (ny - 1), a >> (1 + lrow + ly)
    a_from = a_y * crow + a_row * span_rows + a_place * STEPS + a_step
    turn = jnp.where(iota((hrows, hrows), 1) == a_from, 1.0, 0.0)
    lane = iota((crow, LANES), 1)
    stat = []
    for h in range(halves):
        at = slice(h * crow, (h + 1) * crow)
        rows = [
            jnp.where(
                lane == 0,
                cols[at, nx * ny + y : nx * ny + y + 1],
                jnp.where(lane == 1, cols[at, (nx + 1) * ny + y : (nx + 1) * ny + y + 1], 0.0),
            )
            for y in range(ny)
        ]
        stat.append(mm(turn, jnp.concatenate(rows, axis=0), HIGH))
    szs[...] = jnp.transpose(jnp.concatenate(stat, axis=0))[0:2, :]
    for k in far_first(nz):
        send(szs, szr.at[k - 1], "azs", k - 1, z_dev(k))
    turn = turn.astype(BF16)
    for h in range(halves):
        for kx, ky in reversed(xy_far):
            slot = (kx * ny + ky - 1) * halves + h
            receive(oxr.at[kx, y_of(ny - ky), h], "a", slot, xy_dev(kx, ky))
        at = slice(h * crow, (h + 1) * crow)
        sums = []
        for y in range(ny):
            acc = cols[at, y : y + 1] * oxr[0, y, h].astype(F32)
            for kx in range(1, nx):
                c = kx * ny + y
                acc = acc + cols[at, c : c + 1] * oxr[kx, y, h].astype(F32)
            sums.append(acc.astype(BF16))
        turned = mm(turn, jnp.concatenate(sums, axis=0)).astype(BF16)
        for p in range(per):
            place = h * per + p
            ozs[place] = turned[p * pn.block : (p + 1) * pn.block, :]
            k = zorder[place]
            if k > 0:
                send(ozs.at[place], ozr.at[k - 1], "az", k - 1, z_dev(k))

    receive(ops.at[1 - core], "op", 0, core_dev)
    for z in range(nz):
        for x in range(nx):
            c = z * nx + x
            for half in range(2):
                piece = ops[half, :, c * pn.feat : (c + 1) * pn.feat]
                opw[x, z, half * pn.vrows : (half + 1) * pn.vrows, :] = pad_lanes(
                    piece, pn.featp
                )
    for k in range(1, ne):
        receive(ra.at[e_of(ne - k)], "res", k - 1, e_dev(k))
    lt = log2(pn.tok)

    def owner_of(n):
        y = (n >> lt) & (ny - 1)
        return 2 * y + (n >> (lt + ly)), n & (pn.tok - 1)

    n_row = iota((pn.total, ne * 16), 0)
    n_owner, n_tok = owner_of(n_row)
    spread = iota((pn.total, ne * 16), 1)
    pick = jnp.where(spread == n_owner * 16 + n_tok, 1.0, 0.0).astype(BF16)
    residual = mm(pick, ra[...].reshape(ne * 16, pn.featp))
    vu_copy.wait()

    def stat_of(ref, k):
        at = zorder.index(k) * pn.block
        return pad_lanes(ref[0:2, at : at + pn.block], LANES)

    for k in range(1, nz):
        receive(szr.at[k - 1], "azs", k - 1, z_dev(k))
    stat = [stat_of(szs, 0)] + [stat_of(szr.at[k - 1], k) for k in range(1, nz)]
    coefs, _, _ = joined([s[0:1, :] for s in stat], [s[1:2, :] for s in stat])
    cols = jnp.transpose(pad_rows(jnp.concatenate(coefs, axis=0), LANES))[0 : pn.block, :]
    acc = cols[:, 0:1] * ozs[nz - 1].astype(F32)
    for k in reversed(far_first(nz)):
        receive(ozr.at[k - 1], "az", k - 1, z_dev(k))
        acc = acc + cols[:, k : k + 1] * ozr[k - 1].astype(F32)
    values = mm(acc.astype(BF16), vus[...]).astype(BF16)

    each = nz // pn.parts

    def partner_chunk(h):
        return pl.ds(h * each, each)

    for h in range(pn.parts):
        for k in xorder:
            for p in range(each):
                place = h * each + p
                block = mm(values, opw[x_of(k), z_of(zorder[place])])
                cs[k, place] = block.astype(BF16)
            if k > 0:
                send(
                    cs.at[k, partner_chunk(h)],
                    cr.at[k - 1, partner_chunk(h)],
                    "cx",
                    (k - 1) * pn.parts + h,
                    x_dev(k),
                )
    for h in range(pn.parts):
        for k in range(1, nx):
            receive(
                cr.at[k - 1, partner_chunk(h)], "cx", (k - 1) * pn.parts + h, x_dev(k)
            )
        for p in range(each):
            place = h * each + p
            acc = cs[0, place].astype(F32)
            for i in range(1, nx):
                acc = acc + cr[i - 1, place].astype(F32)
            zs[place] = acc.astype(BF16)
            k = zorder[place]
            if k > 0:
                send(zs.at[place], zr.at[k - 1], "cz", k - 1, z_dev(k))
    acc = zs[nz - 1].astype(F32)
    for k in reversed(far_first(nz)):
        receive(zr.at[k - 1], "cz", k - 1, z_dev(k))
        acc = acc + zr[k - 1].astype(F32)
    ys[...] = acc.astype(BF16)
    for k in far_first(ne):
        send(ys, yr.at[me], "ce", k - 1, e_dev(k))
    yr[me] = ys[...]
    for k in range(1, ne):
        receive(yr.at[e_of(ne - k)], "ce", k - 1, e_dev(k))
    sides = []
    for c in range(2):
        acc = yr[c].astype(F32)
        for y in range(1, ny):
            acc = acc + yr[2 * y + c].astype(F32)
        sides.append(acc)
    hidden = (residual + jnp.concatenate(sides, axis=0)).astype(BF16)
    hidden_f = hidden.astype(F32)

    scaled = (hidden_f[:, 0 : pn.feat] * gain_ref[...].reshape(1, pn.feat)).astype(BF16)
    pltpu.make_async_copy(gus, gus, gu_sem).wait()
    fb = pn.fb
    for h in range(pn.parts):
        for k in xorder:
            for p in range(each):
                place = h * each + p
                block = mm(scaled, gus[x_of(k), z_of(zorder[place])])
                es[k, place] = block.astype(BF16)
            if k > 0:
                send(
                    es.at[k, partner_chunk(h)],
                    exr.at[k - 1, partner_chunk(h)],
                    "ex",
                    (k - 1) * pn.parts + h,
                    x_dev(k),
                )
        if h == 0:
            squares = jnp.sum(hidden_f * hidden_f, axis=1, keepdims=True)
            squares = pad_rows(jnp.broadcast_to(squares, (pn.total, LANES)), LANES)
            qxs[...] = jnp.transpose(squares)[0:2, :]
            for k in far_first(nx):
                send(qxs, qxr.at[k - 1], "sx", k - 1, x_dev(k))
    acc = qxs[...]
    for k in range(1, nx):
        receive(qxr.at[k - 1], "sx", k - 1, x_dev(k))
        acc = acc + qxr[k - 1]
    qzs[...] = acc
    for h in range(pn.parts):
        for k in range(1, nx):
            receive(
                exr.at[k - 1, partner_chunk(h)], "ex", (k - 1) * pn.parts + h, x_dev(k)
            )
        for p in range(each):
            place = h * each + p
            acc = es[0, place].astype(F32)
            for i in range(1, nx):
                acc = acc + exr[i - 1, place].astype(F32)
            ezs[place] = acc.astype(BF16)
            k = zorder[place]
            if k > 0:
                send(ezs.at[place], ezr.at[k - 1], "ez", k - 1, z_dev(k))
                send(qzs, qzr.at[k - 1], "sz", k - 1, z_dev(k))
    acc = qzs[...]
    for k in range(1, nz):
        receive(qzr.at[k - 1], "sz", k - 1, z_dev(k))
        acc = acc + qzr[k - 1]
    scale_row = lax.rsqrt(acc / pn.model + norm_eps)
    scale = jnp.transpose(pad_rows(scale_row, LANES))[0 : pn.total, 0:1]
    acc = ezs[nz - 1].astype(F32)
    for k in reversed(far_first(nz)):
        receive(ezr.at[k - 1], "ez", k - 1, z_dev(k))
        acc = acc + ezr[k - 1].astype(F32)
    acc = acc * scale
    gate, up = acc[:, 0:fb], acc[:, fb : 2 * fb]
    activated = gate / (1.0 + jnp.exp(-gate)) * up
    act[my_x, my_z] = activated.astype(BF16)

    for k in far_first(nz):
        send(act.at[my_x, my_z], act.at[my_x, my_z], "gz", k - 1, z_dev(k))
    dn_copy.wait()
    for k in [0] + list(reversed(far_first(nz))):
        block = act.at[my_x, z_of(nz - k)]
        if k > 0:
            receive(block, "gz", k - 1, z_dev(k))
        for i in far_first(nx):
            send(block, block, "gx", (i - 1) * nz + k, x_dev(i))
    depth = pn.nzz * fb
    outs = [jnp.zeros((pn.total, pn.feat), F32) for _ in range(pn.experts)]
    for k in [0] + list(reversed(far_first(nx))):
        xp = x_of(nx - k)
        if k > 0:
            for i in range(nz):
                receive(act.at[xp, z_of(nz - i)], "gx", (k - 1) * nz + i, x_dev(k))
        for j in range(pn.experts):
            rows = jnp.concatenate(
                [act[xp, j * pn.nzz + zz] for zz in range(pn.nzz)], axis=1
            )
            down = dns[j, :, pl.ds(pl.multiple_of(xp * depth, depth), depth)]
            outs[j] = outs[j] + mm_nt(rows, down)

    s_row = iota((ne * 16, pn.total), 0)
    s_owner, s_tok = owner_of(iota((ne * 16, pn.total), 1))
    acc = jnp.zeros((ne * 16, pn.featp), F32)
    for j in range(pn.experts):
        put = jnp.where(s_row == s_owner * 16 + j * pn.tok + s_tok, 1.0, 0.0).astype(BF16)
        acc = acc + mm(put, pad_lanes(outs[j], pn.featp).astype(BF16))
    fs[...] = acc.astype(BF16).reshape(ne, 16, pn.featp)
    for k in far_first(ne):
        send(fs.at[e_of(k)], fr.at[me], "f", k - 1, e_dev(k))
    fr[me] = fs[me]

    ids = pad_rows(jnp.concatenate([ids_ref[r] for r in range(pn.rows)], axis=0), 8)
    coef = pad_rows(jnp.concatenate([rw_ref[r] for r in range(pn.rows)], axis=0), 8)
    c_row, c_col = iota((8, ne * 16), 0), iota((8, ne * 16), 1)
    place = c_col & 15
    expert = (c_col >> 4) * pn.experts + (place >> lt)
    used = (place < pn.experts * pn.tok) & ((place & (pn.tok - 1)) == c_row)
    mix = jnp.zeros((8, ne * 16), F32)
    for t in range(TOPK):
        mix = mix + jnp.where(used & (expert == ids[:, t : t + 1]), coef[:, t : t + 1], 0.0)
    own_row, own_col = iota((8, pn.total), 0), iota((8, pn.total), 1)
    own_at = core * (pn.total // 2) + my_y * pn.tok + own_row
    own = jnp.where((own_col == own_at) & (own_row < pn.tok), 1.0, 0.0).astype(BF16)
    own_hidden = mm(own, hidden)

    for copy in pending[: 1 - ne]:
        copy.wait_send()
    for k in range(1, ne):
        receive(fr.at[e_of(ne - k)], "f", k - 1, e_dev(k))
    returned = fr[...].reshape(ne * 16, pn.featp).astype(F32)
    mixed = own_hidden + mm(mix, returned, HIGH)
    for r in range(pn.rows):
        out_ref[r] = mixed[r * STEPS : (r + 1) * STEPS, 0 : pn.feat].astype(BF16)
    for copy in pending[1 - ne :]:
        copy.wait_send()


def on_device(
    nx,
    queries,
    new_latent,
    cache,
    lengths,
    value_up,
    out_proj,
    residual,
    norm_gain,
    route_ids,
    route_weights,
    gate_up,
    expert_down,
):
    ne = lax.axis_size("exp")
    nz = lax.axis_size("ctx") // nx
    pn = Plan(nx, nz, ne, queries, cache, out_proj, gate_up)
    keys = pn.span + LANES
    stat_lanes = nz * pn.block
    any_spec = pl.BlockSpec(memory_space=pl.ANY)
    vmem_spec = pl.BlockSpec(memory_space=pltpu.VMEM)
    fp, total = pn.featp, pn.total
    v = pltpu.VMEM
    crow = pn.rows * STEPS * pn.per
    scratch = [
        v(new_latent.shape, BF16),
        pltpu.SMEM(lengths.shape, jnp.int32),
        v(residual.shape, BF16),
        v(norm_gain.shape, F32),
        v(route_ids.shape, jnp.int32),
        v(route_weights.shape, F32),
        v((pn.rows, STEPS, pn.width, pn.heads), BF16),
        v((pn.rows, pn.width, keys), BF16),
        v(value_up.shape[1:], BF16),
        v((2, *out_proj.shape), BF16),
        v((nx, nz, pn.feat, 2 * pn.fb), BF16),
        v((pn.experts, pn.feat, pn.ffe), BF16),
        v((nx, nz, 2 * pn.vrows, fp), BF16),
        v((16, fp), BF16),
        v((ne, 16, fp), BF16),
        v((nx, pn.hl, pn.halves, crow, LATENT), BF16),
        v((nx, pn.ny, pn.halves, crow, LATENT), BF16),
        v((nx, 2, stat_lanes), F32),
        v((nx, pn.ny, 2, stat_lanes), F32),
        v((nz, pn.block, LATENT), BF16),
        v((nz - 1, pn.block, LATENT), BF16),
        v((2, stat_lanes), F32),
        v((nz - 1, 2, stat_lanes), F32),
        v((stat_lanes, LANES), F32),
        v((nx, nz, total // 2, fp), BF16),
        v((nx - 1, nz, total // 2, fp), BF16),
        v((nz, total // 2, fp), BF16),
        v((nz - 1, total // 2, fp), BF16),
        v((total // 2, fp), BF16),
        v((ne, total // 2, fp), BF16),
        v((2, LANES), F32),
        v((nx - 1, 2, LANES), F32),
        v((2, LANES), F32),
        v((nz - 1, 2, LANES), F32),
        v((nx, nz, total, 2 * pn.fb), BF16),
        v((nx - 1, nz, total, 2 * pn.fb), BF16),
        v((nz, total, 2 * pn.fb), BF16),
        v((nz - 1, total, 2 * pn.fb), BF16),
        v((nx, nz, total, pn.fb), BF16),
        v((ne, 16, fp), BF16),
        v((ne, 16, fp), BF16),
        pltpu.SemaphoreType.DMA((pn.n_remote,)),
        pltpu.SemaphoreType.DMA((pn.n_remote,)),
        pltpu.SemaphoreType.DMA((pn.n_local,)),
    ]
    return pl.pallas_call(
        functools.partial(kernel, pn),
        out_shape=jax.ShapeDtypeStruct(residual.shape, BF16),
        in_specs=[any_spec] * 12,
        out_specs=vmem_spec,
        scratch_shapes=scratch,
        compiler_params=pltpu.CompilerParams(
            collective_id=0, has_side_effects=True, vmem_limit_bytes=60 * 1024 * 1024
        ),
        name="decode_layer",
    )(
        jnp.swapaxes(queries, 2, 3),
        new_latent,
        jnp.swapaxes(cache, 1, 2),
        lengths,
        value_up,
        out_proj,
        residual,
        norm_gain,
        route_ids,
        route_weights,
        gate_up,
        jnp.swapaxes(expert_down, 1, 2),
    )


def solution(mesh, nx=CHIPS_X):
    in_specs = (
        P("exp", None, None, None),
        P("exp", None, None),
        P("exp", "ctx", None),
        P("exp"),
        P("ctx", None, None),
        P(("ctx", "exp"), None),
        P("exp", None, "ctx"),
        P("ctx"),
        P("exp", None, None),
        P("exp", None, None),
        P("exp", "ctx", None),
        P("exp", None, "ctx"),
    )
    return jax.shard_map(
        functools.partial(on_device, nx),
        mesh=mesh,
        in_specs=in_specs,
        out_specs=P("exp", None, "ctx"),
        check_vma=False,
    )
```

```python
import functools
import math

import jax
import jax.numpy as jnp
from jax import lax
from jax.experimental import pallas as pl
from jax.experimental.pallas import tpu as pltpu
from jax.sharding import PartitionSpec as P

STEPS = 2
LATENT = 512
VDIM = 128
TOPK = 8
CHIPS_X = 4
LANES = 128

qk_scale = 1.0 / math.sqrt(192.0)
norm_eps = 1e-06
MESH = pl.DeviceIdType.MESH
F32 = jnp.float32
BF16 = jnp.bfloat16
HIGH = lax.Precision.HIGHEST


def iota(shape, dim):
    return lax.broadcasted_iota(jnp.int32, shape, dim)


def log2(n):
    assert n & (n - 1) == 0
    return n.bit_length() - 1


def mm(a, b, precision=None):
    return jnp.dot(a, b, preferred_element_type=F32, precision=precision)


def mm_nt(a, b):
    return lax.dot_general(a, b, (((1,), (1,)), ((), ())), preferred_element_type=F32)


def far_first(n):
    return sorted(range(1, n), key=lambda k: (-min(k, n - k), k))


def pad_lanes(a, width):
    return jnp.concatenate([a, jnp.zeros((a.shape[0], width - a.shape[1]), a.dtype)], axis=1)


def pad_rows(a, height):
    return jnp.concatenate([a, jnp.zeros((height - a.shape[0], a.shape[1]), a.dtype)], axis=0)


class Plan:
    def __init__(self, nx, nz, ne, queries, cache, out_proj, gate_up):
        self.nx, self.nz, self.ne, self.ny = nx, nz, ne, ne // 2
        self.rows = queries.shape[0]
        self.heads = queries.shape[2]
        self.width = queries.shape[3]
        self.span = cache.shape[1]
        self.hl = self.heads // (nx * nz)
        assert self.hl == self.ny
        self.tok = self.rows * STEPS
        self.block = self.tok * self.hl
        self.total = self.tok * ne
        self.model = out_proj.shape[1]
        self.feat = self.model // (nx * nz)
        self.featp = -(-self.feat // LANES) * LANES
        self.vrows = out_proj.shape[0]
        self.ffe = gate_up.shape[2] // 2
        self.experts = gate_up.shape[0]
        self.nzz = nz // self.experts
        self.fb = self.ffe // (nx * self.nzz)
        self.zorder = far_first(nz) + [0]
        self.xorder = far_first(nx) + [0]
        self.halves = 2
        self.parts = min(4, nz)
        self.per = nz // self.halves
        nxy = nx * self.ny - 1
        self.base, at = {}, 0
        for name, n in (
            ("res", ne - 1),
            ("op", 1),
            ("as", nxy),
            ("a", nxy * self.halves),
            ("azs", nz - 1),
            ("az", nz - 1),
            ("cx", (nx - 1) * self.parts),
            ("cz", nz - 1),
            ("ce", ne - 1),
            ("sx", nx - 1),
            ("sz", nz - 1),
            ("ex", (nx - 1) * self.parts),
            ("ez", nz - 1),
            ("gz", nz - 1),
            ("gx", (nx - 1) * nz),
            ("f", ne - 1),
        ):
            self.base[name] = at
            at += n
        self.n_remote = at
        self.n_local = 2 * self.rows + 12


def joined(tops, totals):
    top = functools.reduce(jnp.maximum, tops)
    raw = [d * jnp.exp(p - top) for p, d in zip(tops, totals)]
    total = functools.reduce(jnp.add, raw)
    inv = jnp.where(total > 0.0, 1.0 / jnp.where(total > 0.0, total, 1.0), 0.0)
    return [r * inv for r in raw], top, total


def kernel(
    pn,
    q_hbm,
    nl_hbm,
    cache_hbm,
    len_hbm,
    vu_hbm,
    op_hbm,
    res_hbm,
    gain_hbm,
    ids_hbm,
    rw_hbm,
    gu_hbm,
    dn_hbm,
    out_ref,
    nl_ref,
    len_ref,
    res_ref,
    gain_ref,
    ids_ref,
    rw_ref,
    qs,
    ks,
    vus,
    ops,
    gus,
    dns,
    opw,
    rb,
    ra,
    os_,
    oxr,
    sxs,
    sxr,
    ozs,
    ozr,
    szs,
    szr,
    xy_cols,
    cs,
    cr,
    zs,
    zr,
    ys,
    yr,
    qxs,
    qxr,
    qzs,
    qzr,
    es,
    exr,
    ezs,
    ezr,
    act,
    fs,
    fr,
    send_sems,
    recv_sems,
    local_sems,
):
    nx, ny, nz, ne = pn.nx, pn.ny, pn.nz, pn.ne
    halves, per = pn.halves, pn.per
    zorder, xorder = pn.zorder, pn.xorder
    ctx = lax.axis_index("ctx")
    me = lax.axis_index("exp")
    my_z, my_x = ctx // nx, lax.rem(ctx, nx)
    my_y, core = me // 2, lax.rem(me, 2)
    pending = []

    def x_of(k):
        return lax.rem(my_x + k, nx)

    def y_of(k):
        return lax.rem(my_y + k, ny)

    def z_of(k):
        return lax.rem(my_z + k, nz)

    def e_of(k):
        return lax.rem(me + k, ne)

    def x_dev(k):
        return (my_z * nx + x_of(k), me)

    def xy_dev(kx, ky):
        return (my_z * nx + x_of(kx), 2 * y_of(ky) + core)

    def z_dev(k):
        return (z_of(k) * nx + my_x, me)

    def e_dev(k):
        return (ctx, e_of(k))

    core_dev = (ctx, me + 1 - 2 * core)

    local_at = [0]

    def local(src, dst):
        copy = pltpu.make_async_copy(src, dst, local_sems.at[local_at[0]])
        local_at[0] += 1
        copy.start()
        return copy

    q_copies, k_copies = [], []
    for r in range(pn.rows):
        q_copies.append(local(q_hbm.at[r], qs.at[r]))
        k_copies.append(local(cache_hbm.at[r], ks.at[r, :, pl.ds(0, pn.span)]))
    small_copies = [
        local(nl_hbm, nl_ref),
        local(len_hbm, len_ref),
        local(res_hbm, res_ref),
        local(ids_hbm, ids_ref),
        local(rw_hbm, rw_ref),
        local(gain_hbm, gain_ref),
    ]

    xy_far = [
        (kx, ky) for kx in far_first(nx) + [0] for ky in far_first(ny) + [0] if kx or ky
    ]
    barrier = pltpu.get_barrier_semaphore()
    def hops(k, n):
        return min(k, n - k)

    reached = [(hops(k, nz), z_dev(k)) for k in far_first(nz)]
    reached += [(hops(kx, nx) + hops(ky, ny), xy_dev(kx, ky)) for kx, ky in xy_far]
    reached += [(hops(ky, ny), (ctx, 2 * y_of(ky) + 1 - core)) for ky in range(ny)]
    peers = [dev for _, dev in sorted(reached, key=lambda item: -item[0])]
    for dev in peers:
        pl.semaphore_signal(barrier, inc=1, device_id=dev, device_id_type=MESH)

    def remote(src, dst, name, slot, dev):
        at = pn.base[name] + slot
        return pltpu.make_async_remote_copy(
            src_ref=src,
            dst_ref=dst,
            send_sem=send_sems.at[at],
            recv_sem=recv_sems.at[at],
            device_id=dev,
            device_id_type=MESH,
        )

    def send(src, dst, name, slot, dev):
        copy = remote(src, dst, name, slot, dev)
        copy.start()
        pending.append(copy)

    def receive(dst, name, slot, dev):
        remote(dst, dst, name, slot, dev).wait_recv()

    qrows = STEPS * pn.heads
    keys = pn.span + LANES
    lp, lh, lhl = log2(per), log2(halves), log2(pn.hl)
    m = iota((qrows, qrows), 0)
    m_place = (m >> 1) & (nz - 1)
    m_head = (m >> (1 + lp + lh)) & (pn.hl - 1)
    m_x = m >> (1 + lp + lh + lhl)
    m_z = jnp.zeros_like(m)
    for place, k in enumerate(zorder):
        m_z = jnp.where(m_place == place, z_of(k), m_z)
    source = (m & (STEPS - 1)) * pn.heads + (m_z * nx + m_x) * pn.hl + m_head
    perm = jnp.where(iota((qrows, qrows), 1) == source, 1.0, 0.0).astype(BF16)

    col = iota((qrows, keys), 1)
    step = iota((qrows, keys), 0) & (STEPS - 1)
    first = jnp.where(ctx == 0, 0, -LANES)
    is_fresh = (col >= pn.span) & (col - pn.span <= step + first)
    position = ctx * pn.span + col

    for copy in small_copies:
        copy.wait()
    for r in range(pn.rows):
        fresh = pad_lanes(nl_ref[r].astype(F32), -(-pn.width // LANES) * LANES)
        fresh = jnp.transpose(pad_rows(fresh, LANES))[0 : pn.width, :]
        ks[r, :, pl.ds(pn.span, LANES)] = fresh.astype(BF16)
    res_rows = jnp.concatenate([res_ref[r].astype(F32) for r in range(pn.rows)], axis=0)
    rb[...] = pad_rows(pad_lanes(res_rows, pn.featp), 16).astype(BF16)
    ra[me] = rb[...]

    for copy in q_copies + k_copies:
        copy.wait()
    every = range(pn.rows)
    turned = [
        functools.reduce(
            jnp.add,
            [
                mm_nt(perm[:, s * pn.heads : (s + 1) * pn.heads], qs[r, s])
                for s in range(STEPS)
            ],
        ).astype(BF16)
        for r in every
    ]
    scores = [mm(turned[r], ks[r]) for r in every]
    visible = [
        ((col < pn.span) & (position < len_ref[r])) | is_fresh for r in every
    ]
    scores = [jnp.where(visible[r], scores[r] * qk_scale, -1e30) for r in every]
    peaks = [jnp.max(s, axis=1, keepdims=True) for s in scores]
    weights = [
        jnp.where(visible[r], jnp.exp(scores[r] - peaks[r]), 0.0) for r in every
    ]
    denoms = [jnp.sum(w, axis=1, keepdims=True) for w in weights]
    mixtures = [
        mm_nt(weights[r].astype(BF16), ks[r, pl.ds(0, LATENT), :]) for r in every
    ]
    partial = [
        mixtures[r]
        * jnp.where(denoms[r] > 0.0, 1.0 / jnp.where(denoms[r] > 0.0, denoms[r], 1.0), 0.0)
        for r in every
    ]

    span_rows = STEPS * per
    groups = nx * pn.hl * halves
    crow = pn.rows * span_rows
    merged = jnp.concatenate(
        [p.reshape(groups, span_rows, LATENT) for p in partial], axis=1
    )
    os_[...] = merged.astype(BF16).reshape(nx, pn.hl, halves, crow, LATENT)

    def send_partial(h):
        for kx, ky in xy_far:
            send(
                os_.at[x_of(kx), y_of(ky), h],
                oxr.at[kx, my_y, h],
                "a",
                (kx * ny + ky - 1) * halves + h,
                xy_dev(kx, ky),
            )

    pl.semaphore_wait(barrier, len(peers))
    send_partial(0)
    lane = iota((qrows, LANES), 1)
    stat = [
        jnp.where(lane == 0, p, jnp.where(lane == 1, d, 0.0)) for p, d in zip(peaks, denoms)
    ]
    stat = jnp.concatenate([s.reshape(groups, span_rows, LANES) for s in stat], axis=1)
    stat = stat.reshape(nx, nz * pn.block, LANES)
    for x in range(nx):
        sxs[x] = jnp.transpose(stat[x])[0:2, :]
    for kx, ky in xy_far:
        slot = kx * ny + ky - 1
        send(sxs.at[x_of(kx)], sxr.at[kx, my_y], "as", slot, xy_dev(kx, ky))
    for h in range(1, halves):
        send_partial(h)
    sxr[0, my_y] = sxs[my_x]
    oxr[0, my_y] = os_[my_x, my_y]
    op_copy = local(op_hbm, ops.at[core])
    vu_copy = local(vu_hbm.at[my_y], vus)
    gu_sem = local_sems.at[pn.n_local - 1]
    for x in range(nx):
        for z in range(nz):
            j, zz = z // pn.nzz, z % pn.nzz
            for g in range(2):
                at = g * pn.ffe + (x * pn.nzz + zz) * pn.fb
                pltpu.make_async_copy(
                    gu_hbm.at[j, :, pl.ds(at, pn.fb)],
                    gus.at[x, z, :, pl.ds(g * pn.fb, pn.fb)],
                    gu_sem,
                ).start()
    dn_copy = local(dn_hbm, dns)
    op_copy.wait()
    send(ops.at[core], ops.at[core], "op", 0, core_dev)
    for k in range(1, ne):
        send(rb, ra.at[me], "res", k - 1, e_dev(k))

    for kx, ky in reversed(xy_far):
        src_y = y_of(ny - ky)
        receive(sxr.at[kx, src_y], "as", kx * ny + ky - 1, xy_dev(kx, ky))
    tops = [
        jnp.concatenate([sxr[kx, y, 0:1, :] for y in range(ny)], axis=0) for kx in range(nx)
    ]
    totals = [
        jnp.concatenate([sxr[kx, y, 1:2, :] for y in range(ny)], axis=0) for kx in range(nx)
    ]
    coefs, top, total = joined(tops, totals)
    table = pad_rows(jnp.concatenate(coefs + [top, total], axis=0), LANES)
    xy_cols[...] = jnp.transpose(table)
    mine = halves * crow
    cols = xy_cols[pl.ds(pl.multiple_of(my_y * mine, mine), mine), :]

    hrows = ny * crow
    lrow, ly = log2(pn.rows), log2(ny)
    a = iota((hrows, hrows), 0)
    a_step, a_row = a & 1, (a >> 1) & (pn.rows - 1)
    a_y, a_place = (a >> (1 + lrow)) & (ny - 1), a >> (1 + lrow + ly)
    a_from = a_y * crow + a_row * span_rows + a_place * STEPS + a_step
    turn = jnp.where(iota((hrows, hrows), 1) == a_from, 1.0, 0.0)
    lane = iota((crow, LANES), 1)
    stat = []
    for h in range(halves):
        at = slice(h * crow, (h + 1) * crow)
        rows = [
            jnp.where(
                lane == 0,
                cols[at, nx * ny + y : nx * ny + y + 1],
                jnp.where(lane == 1, cols[at, (nx + 1) * ny + y : (nx + 1) * ny + y + 1], 0.0),
            )
            for y in range(ny)
        ]
        stat.append(mm(turn, jnp.concatenate(rows, axis=0), HIGH))
    szs[...] = jnp.transpose(jnp.concatenate(stat, axis=0))[0:2, :]
    for k in far_first(nz):
        send(szs, szr.at[k - 1], "azs", k - 1, z_dev(k))
    turn = turn.astype(BF16)
    for h in range(halves):
        for kx, ky in reversed(xy_far):
            slot = (kx * ny + ky - 1) * halves + h
            receive(oxr.at[kx, y_of(ny - ky), h], "a", slot, xy_dev(kx, ky))
        at = slice(h * crow, (h + 1) * crow)
        sums = []
        for y in range(ny):
            acc = cols[at, y : y + 1] * oxr[0, y, h].astype(F32)
            for kx in range(1, nx):
                c = kx * ny + y
                acc = acc + cols[at, c : c + 1] * oxr[kx, y, h].astype(F32)
            sums.append(acc.astype(BF16))
        turned = mm(turn, jnp.concatenate(sums, axis=0)).astype(BF16)
        for p in range(per):
            place = h * per + p
            ozs[place] = turned[p * pn.block : (p + 1) * pn.block, :]
            k = zorder[place]
            if k > 0:
                send(ozs.at[place], ozr.at[k - 1], "az", k - 1, z_dev(k))

    receive(ops.at[1 - core], "op", 0, core_dev)
    for z in range(nz):
        for x in range(nx):
            c = z * nx + x
            for half in range(2):
                piece = ops[half, :, c * pn.feat : (c + 1) * pn.feat]
                opw[x, z, half * pn.vrows : (half + 1) * pn.vrows, :] = pad_lanes(
                    piece, pn.featp
                )
    for k in range(1, ne):
        receive(ra.at[e_of(ne - k)], "res", k - 1, e_dev(k))
    lt = log2(pn.tok)

    def owner_of(n):
        y = (n >> lt) & (ny - 1)
        return 2 * y + (n >> (lt + ly)), n & (pn.tok - 1)

    n_row = iota((pn.total, ne * 16), 0)
    n_owner, n_tok = owner_of(n_row)
    spread = iota((pn.total, ne * 16), 1)
    pick = jnp.where(spread == n_owner * 16 + n_tok, 1.0, 0.0).astype(BF16)
    residual = mm(pick, ra[...].reshape(ne * 16, pn.featp))
    vu_copy.wait()

    def stat_of(ref, k):
        at = zorder.index(k) * pn.block
        return pad_lanes(ref[0:2, at : at + pn.block], LANES)

    for k in range(1, nz):
        receive(szr.at[k - 1], "azs", k - 1, z_dev(k))
    stat = [stat_of(szs, 0)] + [stat_of(szr.at[k - 1], k) for k in range(1, nz)]
    coefs, _, _ = joined([s[0:1, :] for s in stat], [s[1:2, :] for s in stat])
    cols = jnp.transpose(pad_rows(jnp.concatenate(coefs, axis=0), LANES))[0 : pn.block, :]
    acc = cols[:, 0:1] * ozs[nz - 1].astype(F32)
    for k in reversed(far_first(nz)):
        receive(ozr.at[k - 1], "az", k - 1, z_dev(k))
        acc = acc + cols[:, k : k + 1] * ozr[k - 1].astype(F32)
    values = mm(acc.astype(BF16), vus[...]).astype(BF16)

    each = nz // pn.parts

    def partner_chunk(h):
        return pl.ds(h * each, each)

    for h in range(pn.parts):
        for k in xorder:
            for p in range(each):
                place = h * each + p
                block = mm(values, opw[x_of(k), z_of(zorder[place])])
                cs[k, place] = block.astype(BF16)
            if k > 0:
                send(
                    cs.at[k, partner_chunk(h)],
                    cr.at[k - 1, partner_chunk(h)],
                    "cx",
                    (k - 1) * pn.parts + h,
                    x_dev(k),
                )
    for h in range(pn.parts):
        for k in range(1, nx):
            receive(
                cr.at[k - 1, partner_chunk(h)], "cx", (k - 1) * pn.parts + h, x_dev(k)
            )
        for p in range(each):
            place = h * each + p
            acc = cs[0, place].astype(F32)
            for i in range(1, nx):
                acc = acc + cr[i - 1, place].astype(F32)
            zs[place] = acc.astype(BF16)
            k = zorder[place]
            if k > 0:
                send(zs.at[place], zr.at[k - 1], "cz", k - 1, z_dev(k))
    acc = zs[nz - 1].astype(F32)
    for k in reversed(far_first(nz)):
        receive(zr.at[k - 1], "cz", k - 1, z_dev(k))
        acc = acc + zr[k - 1].astype(F32)
    ys[...] = acc.astype(BF16)
    for k in far_first(ne):
        send(ys, yr.at[me], "ce", k - 1, e_dev(k))
    yr[me] = ys[...]
    for k in range(1, ne):
        receive(yr.at[e_of(ne - k)], "ce", k - 1, e_dev(k))
    sides = []
    for c in range(2):
        acc = yr[c].astype(F32)
        for y in range(1, ny):
            acc = acc + yr[2 * y + c].astype(F32)
        sides.append(acc)
    hidden = (residual + jnp.concatenate(sides, axis=0)).astype(BF16)
    hidden_f = hidden.astype(F32)

    scaled = (hidden_f[:, 0 : pn.feat] * gain_ref[...].reshape(1, pn.feat)).astype(BF16)
    pltpu.make_async_copy(gus, gus, gu_sem).wait()
    fb = pn.fb
    for h in range(pn.parts):
        for k in xorder:
            for p in range(each):
                place = h * each + p
                block = mm(scaled, gus[x_of(k), z_of(zorder[place])])
                es[k, place] = block.astype(BF16)
            if k > 0:
                send(
                    es.at[k, partner_chunk(h)],
                    exr.at[k - 1, partner_chunk(h)],
                    "ex",
                    (k - 1) * pn.parts + h,
                    x_dev(k),
                )
        if h == 0:
            squares = jnp.sum(hidden_f * hidden_f, axis=1, keepdims=True)
            squares = pad_rows(jnp.broadcast_to(squares, (pn.total, LANES)), LANES)
            qxs[...] = jnp.transpose(squares)[0:2, :]
            for k in far_first(nx):
                send(qxs, qxr.at[k - 1], "sx", k - 1, x_dev(k))
    acc = qxs[...]
    for k in range(1, nx):
        receive(qxr.at[k - 1], "sx", k - 1, x_dev(k))
        acc = acc + qxr[k - 1]
    qzs[...] = acc
    for h in range(pn.parts):
        for k in range(1, nx):
            receive(
                exr.at[k - 1, partner_chunk(h)], "ex", (k - 1) * pn.parts + h, x_dev(k)
            )
        for p in range(each):
            place = h * each + p
            acc = es[0, place].astype(F32)
            for i in range(1, nx):
                acc = acc + exr[i - 1, place].astype(F32)
            ezs[place] = acc.astype(BF16)
            k = zorder[place]
            if k > 0:
                send(ezs.at[place], ezr.at[k - 1], "ez", k - 1, z_dev(k))
                send(qzs, qzr.at[k - 1], "sz", k - 1, z_dev(k))
    acc = qzs[...]
    for k in range(1, nz):
        receive(qzr.at[k - 1], "sz", k - 1, z_dev(k))
        acc = acc + qzr[k - 1]
    scale_row = lax.rsqrt(acc / pn.model + norm_eps)
    scale = jnp.transpose(pad_rows(scale_row, LANES))[0 : pn.total, 0:1]
    acc = ezs[nz - 1].astype(F32)
    for k in reversed(far_first(nz)):
        receive(ezr.at[k - 1], "ez", k - 1, z_dev(k))
        acc = acc + ezr[k - 1].astype(F32)
    acc = acc * scale
    gate, up = acc[:, 0:fb], acc[:, fb : 2 * fb]
    activated = gate / (1.0 + jnp.exp(-gate)) * up
    act[my_x, my_z] = activated.astype(BF16)

    for k in far_first(nz):
        send(act.at[my_x, my_z], act.at[my_x, my_z], "gz", k - 1, z_dev(k))
    dn_copy.wait()
    for k in [0] + list(reversed(far_first(nz))):
        block = act.at[my_x, z_of(nz - k)]
        if k > 0:
            receive(block, "gz", k - 1, z_dev(k))
        for i in far_first(nx):
            send(block, block, "gx", (i - 1) * nz + k, x_dev(i))
    depth = pn.nzz * fb
    outs = [jnp.zeros((pn.total, pn.feat), F32) for _ in range(pn.experts)]
    for k in [0] + list(reversed(far_first(nx))):
        xp = x_of(nx - k)
        if k > 0:
            for i in range(nz):
                receive(act.at[xp, z_of(nz - i)], "gx", (k - 1) * nz + i, x_dev(k))
        for j in range(pn.experts):
            rows = jnp.concatenate(
                [act[xp, j * pn.nzz + zz] for zz in range(pn.nzz)], axis=1
            )
            down = dns[j, :, pl.ds(pl.multiple_of(xp * depth, depth), depth)]
            outs[j] = outs[j] + mm_nt(rows, down)

    s_row = iota((ne * 16, pn.total), 0)
    s_owner, s_tok = owner_of(iota((ne * 16, pn.total), 1))
    acc = jnp.zeros((ne * 16, pn.featp), F32)
    for j in range(pn.experts):
        put = jnp.where(s_row == s_owner * 16 + j * pn.tok + s_tok, 1.0, 0.0).astype(BF16)
        acc = acc + mm(put, pad_lanes(outs[j], pn.featp).astype(BF16))
    fs[...] = acc.astype(BF16).reshape(ne, 16, pn.featp)
    for k in far_first(ne):
        send(fs.at[e_of(k)], fr.at[me], "f", k - 1, e_dev(k))
    fr[me] = fs[me]

    ids = pad_rows(jnp.concatenate([ids_ref[r] for r in range(pn.rows)], axis=0), 8)
    coef = pad_rows(jnp.concatenate([rw_ref[r] for r in range(pn.rows)], axis=0), 8)
    c_row, c_col = iota((8, ne * 16), 0), iota((8, ne * 16), 1)
    place = c_col & 15
    expert = (c_col >> 4) * pn.experts + (place >> lt)
    used = (place < pn.experts * pn.tok) & ((place & (pn.tok - 1)) == c_row)
    mix = jnp.zeros((8, ne * 16), F32)
    for t in range(TOPK):
        mix = mix + jnp.where(used & (expert == ids[:, t : t + 1]), coef[:, t : t + 1], 0.0)
    own_row, own_col = iota((8, pn.total), 0), iota((8, pn.total), 1)
    own_at = core * (pn.total // 2) + my_y * pn.tok + own_row
    own = jnp.where((own_col == own_at) & (own_row < pn.tok), 1.0, 0.0).astype(BF16)
    own_hidden = mm(own, hidden)

    for copy in pending[: 1 - ne]:
        copy.wait_send()
    for k in range(1, ne):
        receive(fr.at[e_of(ne - k)], "f", k - 1, e_dev(k))
    returned = fr[...].reshape(ne * 16, pn.featp).astype(F32)
    mixed = own_hidden + mm(mix, returned, HIGH)
    for r in range(pn.rows):
        out_ref[r] = mixed[r * STEPS : (r + 1) * STEPS, 0 : pn.feat].astype(BF16)
    for copy in pending[1 - ne :]:
        copy.wait_send()


def on_device(
    nx,
    queries,
    new_latent,
    cache,
    lengths,
    value_up,
    out_proj,
    residual,
    norm_gain,
    route_ids,
    route_weights,
    gate_up,
    expert_down,
):
    ne = lax.axis_size("exp")
    nz = lax.axis_size("ctx") // nx
    pn = Plan(nx, nz, ne, queries, cache, out_proj, gate_up)
    keys = pn.span + LANES
    stat_lanes = nz * pn.block
    any_spec = pl.BlockSpec(memory_space=pl.ANY)
    vmem_spec = pl.BlockSpec(memory_space=pltpu.VMEM)
    fp, total = pn.featp, pn.total
    v = pltpu.VMEM
    crow = pn.rows * STEPS * pn.per
    scratch = [
        v(new_latent.shape, BF16),
        pltpu.SMEM(lengths.shape, jnp.int32),
        v(residual.shape, BF16),
        v(norm_gain.shape, F32),
        v(route_ids.shape, jnp.int32),
        v(route_weights.shape, F32),
        v((pn.rows, STEPS, pn.width, pn.heads), BF16),
        v((pn.rows, pn.width, keys), BF16),
        v(value_up.shape[1:], BF16),
        v((2, *out_proj.shape), BF16),
        v((nx, nz, pn.feat, 2 * pn.fb), BF16),
        v((pn.experts, pn.feat, pn.ffe), BF16),
        v((nx, nz, 2 * pn.vrows, fp), BF16),
        v((16, fp), BF16),
        v((ne, 16, fp), BF16),
        v((nx, pn.hl, pn.halves, crow, LATENT), BF16),
        v((nx, pn.ny, pn.halves, crow, LATENT), BF16),
        v((nx, 2, stat_lanes), F32),
        v((nx, pn.ny, 2, stat_lanes), F32),
        v((nz, pn.block, LATENT), BF16),
        v((nz - 1, pn.block, LATENT), BF16),
        v((2, stat_lanes), F32),
        v((nz - 1, 2, stat_lanes), F32),
        v((stat_lanes, LANES), F32),
        v((nx, nz, total // 2, fp), BF16),
        v((nx - 1, nz, total // 2, fp), BF16),
        v((nz, total // 2, fp), BF16),
        v((nz - 1, total // 2, fp), BF16),
        v((total // 2, fp), BF16),
        v((ne, total // 2, fp), BF16),
        v((2, LANES), F32),
        v((nx - 1, 2, LANES), F32),
        v((2, LANES), F32),
        v((nz - 1, 2, LANES), F32),
        v((nx, nz, total, 2 * pn.fb), BF16),
        v((nx - 1, nz, total, 2 * pn.fb), BF16),
        v((nz, total, 2 * pn.fb), BF16),
        v((nz - 1, total, 2 * pn.fb), BF16),
        v((nx, nz, total, pn.fb), BF16),
        v((ne, 16, fp), BF16),
        v((ne, 16, fp), BF16),
        pltpu.SemaphoreType.DMA((pn.n_remote,)),
        pltpu.SemaphoreType.DMA((pn.n_remote,)),
        pltpu.SemaphoreType.DMA((pn.n_local,)),
    ]
    return pl.pallas_call(
        functools.partial(kernel, pn),
        out_shape=jax.ShapeDtypeStruct(residual.shape, BF16),
        in_specs=[any_spec] * 12,
        out_specs=vmem_spec,
        scratch_shapes=scratch,
        compiler_params=pltpu.CompilerParams(
            collective_id=0, has_side_effects=True, vmem_limit_bytes=60 * 1024 * 1024
        ),
        name="decode_layer",
    )(
        jnp.swapaxes(queries, 2, 3),
        new_latent,
        jnp.swapaxes(cache, 1, 2),
        lengths,
        value_up,
        out_proj,
        residual,
        norm_gain,
        route_ids,
        route_weights,
        gate_up,
        jnp.swapaxes(expert_down, 1, 2),
    )


def solution(mesh, nx=CHIPS_X):
    in_specs = (
        P("exp", None, None, None),
        P("exp", None, None),
        P("exp", "ctx", None),
        P("exp"),
        P("ctx", None, None),
        P(("ctx", "exp"), None),
        P("exp", None, "ctx"),
        P("ctx"),
        P("exp", None, None),
        P("exp", None, None),
        P("exp", "ctx", None),
        P("exp", None, "ctx"),
    )
    return jax.shard_map(
        functools.partial(on_device, nx),
        mesh=mesh,
        in_specs=in_specs,
        out_specs=P("exp", None, "ctx"),
        check_vma=False,
    )
```

```python
import functools
import math

import jax
import jax.numpy as jnp
from jax import lax
from jax.experimental import pallas as pl
from jax.experimental.pallas import tpu as pltpu
from jax.sharding import PartitionSpec as P

STEPS = 2
LATENT = 512
VDIM = 128
TOPK = 8
CHIPS_X = 4
LANES = 128

qk_scale = 1.0 / math.sqrt(192.0)
norm_eps = 1e-06
MESH = pl.DeviceIdType.MESH
F32 = jnp.float32
BF16 = jnp.bfloat16
HIGH = lax.Precision.HIGHEST


def iota(shape, dim):
    return lax.broadcasted_iota(jnp.int32, shape, dim)


def log2(n):
    assert n & (n - 1) == 0
    return n.bit_length() - 1


def mm(a, b, precision=None):
    return jnp.dot(a, b, preferred_element_type=F32, precision=precision)


def mm_nt(a, b):
    return lax.dot_general(a, b, (((1,), (1,)), ((), ())), preferred_element_type=F32)


def far_first(n):
    return sorted(range(1, n), key=lambda k: (-min(k, n - k), k))


def pad_lanes(a, width):
    return jnp.concatenate([a, jnp.zeros((a.shape[0], width - a.shape[1]), a.dtype)], axis=1)


def pad_rows(a, height):
    return jnp.concatenate([a, jnp.zeros((height - a.shape[0], a.shape[1]), a.dtype)], axis=0)


class Plan:
    def __init__(self, nx, nz, ne, queries, cache, out_proj, gate_up):
        self.nx, self.nz, self.ne, self.ny = nx, nz, ne, ne // 2
        self.rows = queries.shape[0]
        self.heads = queries.shape[2]
        self.width = queries.shape[3]
        self.span = cache.shape[1]
        self.hl = self.heads // (nx * nz)
        assert self.hl == self.ny
        self.tok = self.rows * STEPS
        self.block = self.tok * self.hl
        self.total = self.tok * ne
        self.model = out_proj.shape[1]
        self.feat = self.model // (nx * nz)
        self.featp = -(-self.feat // LANES) * LANES
        self.vrows = out_proj.shape[0]
        self.ffe = gate_up.shape[2] // 2
        self.experts = gate_up.shape[0]
        self.nzz = nz // self.experts
        self.fb = self.ffe // (nx * self.nzz)
        self.zorder = far_first(nz) + [0]
        self.xorder = far_first(nx) + [0]
        self.halves = 2
        self.parts = min(4, nz)
        self.per = nz // self.halves
        nxy = nx * self.ny - 1
        self.base, at = {}, 0
        for name, n in (
            ("res", ne - 1),
            ("op", 1),
            ("as", nxy),
            ("a", nxy * self.halves),
            ("azs", nz - 1),
            ("az", nz - 1),
            ("cx", (nx - 1) * self.parts),
            ("cz", nz - 1),
            ("ce", ne - 1),
            ("sx", nx - 1),
            ("sz", nz - 1),
            ("ex", (nx - 1) * self.parts),
            ("ez", nz - 1),
            ("gz", nz - 1),
            ("gx", (nx - 1) * nz),
            ("f", ne - 1),
        ):
            self.base[name] = at
            at += n
        self.n_remote = at
        self.n_local = 2 * self.rows + 12


def joined(tops, totals):
    top = functools.reduce(jnp.maximum, tops)
    raw = [d * jnp.exp(p - top) for p, d in zip(tops, totals)]
    total = functools.reduce(jnp.add, raw)
    inv = jnp.where(total > 0.0, 1.0 / jnp.where(total > 0.0, total, 1.0), 0.0)
    return [r * inv for r in raw], top, total


def kernel(
    pn,
    q_hbm,
    nl_hbm,
    cache_hbm,
    len_hbm,
    vu_hbm,
    op_hbm,
    res_hbm,
    gain_hbm,
    ids_hbm,
    rw_hbm,
    gu_hbm,
    dn_hbm,
    out_ref,
    nl_ref,
    len_ref,
    res_ref,
    gain_ref,
    ids_ref,
    rw_ref,
    qs,
    ks,
    vus,
    ops,
    gus,
    dns,
    opw,
    rb,
    ra,
    os_,
    oxr,
    sxs,
    sxr,
    ozs,
    ozr,
    szs,
    szr,
    xy_cols,
    cs,
    cr,
    zs,
    zr,
    ys,
    yr,
    qxs,
    qxr,
    qzs,
    qzr,
    es,
    exr,
    ezs,
    ezr,
    act,
    fs,
    fr,
    send_sems,
    recv_sems,
    local_sems,
):
    nx, ny, nz, ne = pn.nx, pn.ny, pn.nz, pn.ne
    halves, per = pn.halves, pn.per
    zorder, xorder = pn.zorder, pn.xorder
    ctx = lax.axis_index("ctx")
    me = lax.axis_index("exp")
    my_z, my_x = ctx // nx, lax.rem(ctx, nx)
    my_y, core = me // 2, lax.rem(me, 2)
    pending = []

    def x_of(k):
        return lax.rem(my_x + k, nx)

    def y_of(k):
        return lax.rem(my_y + k, ny)

    def z_of(k):
        return lax.rem(my_z + k, nz)

    def e_of(k):
        return lax.rem(me + k, ne)

    def x_dev(k):
        return (my_z * nx + x_of(k), me)

    def xy_dev(kx, ky):
        return (my_z * nx + x_of(kx), 2 * y_of(ky) + core)

    def z_dev(k):
        return (z_of(k) * nx + my_x, me)

    def e_dev(k):
        return (ctx, e_of(k))

    core_dev = (ctx, me + 1 - 2 * core)

    local_at = [0]

    def local(src, dst):
        copy = pltpu.make_async_copy(src, dst, local_sems.at[local_at[0]])
        local_at[0] += 1
        copy.start()
        return copy

    q_copies, k_copies = [], []
    for r in range(pn.rows):
        q_copies.append(local(q_hbm.at[r], qs.at[r]))
        k_copies.append(local(cache_hbm.at[r], ks.at[r, :, pl.ds(0, pn.span)]))
    small_copies = [
        local(nl_hbm, nl_ref),
        local(len_hbm, len_ref),
        local(res_hbm, res_ref),
        local(ids_hbm, ids_ref),
        local(rw_hbm, rw_ref),
        local(gain_hbm, gain_ref),
    ]

    xy_far = [
        (kx, ky) for kx in far_first(nx) + [0] for ky in far_first(ny) + [0] if kx or ky
    ]
    barrier = pltpu.get_barrier_semaphore()
    def hops(k, n):
        return min(k, n - k)

    reached = [(hops(k, nz), z_dev(k)) for k in far_first(nz)]
    reached += [(hops(kx, nx) + hops(ky, ny), xy_dev(kx, ky)) for kx, ky in xy_far]
    reached += [(hops(ky, ny), (ctx, 2 * y_of(ky) + 1 - core)) for ky in range(ny)]
    peers = [dev for _, dev in sorted(reached, key=lambda item: -item[0])]
    for dev in peers:
        pl.semaphore_signal(barrier, inc=1, device_id=dev, device_id_type=MESH)

    def remote(src, dst, name, slot, dev):
        at = pn.base[name] + slot
        return pltpu.make_async_remote_copy(
            src_ref=src,
            dst_ref=dst,
            send_sem=send_sems.at[at],
            recv_sem=recv_sems.at[at],
            device_id=dev,
            device_id_type=MESH,
        )

    def send(src, dst, name, slot, dev):
        copy = remote(src, dst, name, slot, dev)
        copy.start()
        pending.append(copy)

    def receive(dst, name, slot, dev):
        remote(dst, dst, name, slot, dev).wait_recv()

    qrows = STEPS * pn.heads
    keys = pn.span + LANES
    lp, lh, lhl = log2(per), log2(halves), log2(pn.hl)
    m = iota((qrows, qrows), 0)
    m_place = (m >> 1) & (nz - 1)
    m_head = (m >> (1 + lp + lh)) & (pn.hl - 1)
    m_x = m >> (1 + lp + lh + lhl)
    m_z = jnp.zeros_like(m)
    for place, k in enumerate(zorder):
        m_z = jnp.where(m_place == place, z_of(k), m_z)
    source = (m & (STEPS - 1)) * pn.heads + (m_z * nx + m_x) * pn.hl + m_head
    perm = jnp.where(iota((qrows, qrows), 1) == source, 1.0, 0.0).astype(BF16)

    col = iota((qrows, keys), 1)
    step = iota((qrows, keys), 0) & (STEPS - 1)
    first = jnp.where(ctx == 0, 0, -LANES)
    is_fresh = (col >= pn.span) & (col - pn.span <= step + first)
    position = ctx * pn.span + col

    for copy in small_copies:
        copy.wait()
    for r in range(pn.rows):
        fresh = pad_lanes(nl_ref[r].astype(F32), -(-pn.width // LANES) * LANES)
        fresh = jnp.transpose(pad_rows(fresh, LANES))[0 : pn.width, :]
        ks[r, :, pl.ds(pn.span, LANES)] = fresh.astype(BF16)
    res_rows = jnp.concatenate([res_ref[r].astype(F32) for r in range(pn.rows)], axis=0)
    rb[...] = pad_rows(pad_lanes(res_rows, pn.featp), 16).astype(BF16)
    ra[me] = rb[...]

    for copy in q_copies + k_copies:
        copy.wait()
    every = range(pn.rows)
    turned = [
        functools.reduce(
            jnp.add,
            [
                mm_nt(perm[:, s * pn.heads : (s + 1) * pn.heads], qs[r, s])
                for s in range(STEPS)
            ],
        ).astype(BF16)
        for r in every
    ]
    scores = [mm(turned[r], ks[r]) for r in every]
    visible = [
        ((col < pn.span) & (position < len_ref[r])) | is_fresh for r in every
    ]
    scores = [jnp.where(visible[r], scores[r] * qk_scale, -1e30) for r in every]
    peaks = [jnp.max(s, axis=1, keepdims=True) for s in scores]
    weights = [
        jnp.where(visible[r], jnp.exp(scores[r] - peaks[r]), 0.0) for r in every
    ]
    denoms = [jnp.sum(w, axis=1, keepdims=True) for w in weights]
    mixtures = [
        mm_nt(weights[r].astype(BF16), ks[r, pl.ds(0, LATENT), :]) for r in every
    ]
    partial = [
        mixtures[r]
        * jnp.where(denoms[r] > 0.0, 1.0 / jnp.where(denoms[r] > 0.0, denoms[r], 1.0), 0.0)
        for r in every
    ]

    span_rows = STEPS * per
    groups = nx * pn.hl * halves
    crow = pn.rows * span_rows
    merged = jnp.concatenate(
        [p.reshape(groups, span_rows, LATENT) for p in partial], axis=1
    )
    os_[...] = merged.astype(BF16).reshape(nx, pn.hl, halves, crow, LATENT)

    def send_partial(h):
        for kx, ky in xy_far:
            send(
                os_.at[x_of(kx), y_of(ky), h],
                oxr.at[kx, my_y, h],
                "a",
                (kx * ny + ky - 1) * halves + h,
                xy_dev(kx, ky),
            )

    lane = iota((qrows, LANES), 1)
    stat = [
        jnp.where(lane == 0, p, jnp.where(lane == 1, d, 0.0)) for p, d in zip(peaks, denoms)
    ]
    stat = jnp.concatenate([s.reshape(groups, span_rows, LANES) for s in stat], axis=1)
    stat = stat.reshape(nx, nz * pn.block, LANES)
    for x in range(nx):
        sxs[x] = jnp.transpose(stat[x])[0:2, :]
    pl.semaphore_wait(barrier, len(peers))
    for kx, ky in xy_far:
        slot = kx * ny + ky - 1
        send(sxs.at[x_of(kx)], sxr.at[kx, my_y], "as", slot, xy_dev(kx, ky))
    send_partial(0)
    for h in range(1, halves):
        send_partial(h)
    sxr[0, my_y] = sxs[my_x]
    oxr[0, my_y] = os_[my_x, my_y]
    op_copy = local(op_hbm, ops.at[core])
    vu_copy = local(vu_hbm.at[my_y], vus)
    gu_sem = local_sems.at[pn.n_local - 1]
    for x in range(nx):
        for z in range(nz):
            j, zz = z // pn.nzz, z % pn.nzz
            for g in range(2):
                at = g * pn.ffe + (x * pn.nzz + zz) * pn.fb
                pltpu.make_async_copy(
                    gu_hbm.at[j, :, pl.ds(at, pn.fb)],
                    gus.at[x, z, :, pl.ds(g * pn.fb, pn.fb)],
                    gu_sem,
                ).start()
    dn_copy = local(dn_hbm, dns)
    op_copy.wait()
    send(ops.at[core], ops.at[core], "op", 0, core_dev)
    for k in range(1, ne):
        send(rb, ra.at[me], "res", k - 1, e_dev(k))

    for kx, ky in reversed(xy_far):
        src_y = y_of(ny - ky)
        receive(sxr.at[kx, src_y], "as", kx * ny + ky - 1, xy_dev(kx, ky))
    tops = [
        jnp.concatenate([sxr[kx, y, 0:1, :] for y in range(ny)], axis=0) for kx in range(nx)
    ]
    totals = [
        jnp.concatenate([sxr[kx, y, 1:2, :] for y in range(ny)], axis=0) for kx in range(nx)
    ]
    coefs, top, total = joined(tops, totals)
    table = pad_rows(jnp.concatenate(coefs + [top, total], axis=0), LANES)
    xy_cols[...] = jnp.transpose(table)
    mine = halves * crow
    cols = xy_cols[pl.ds(pl.multiple_of(my_y * mine, mine), mine), :]

    hrows = ny * crow
    lrow, ly = log2(pn.rows), log2(ny)
    a = iota((hrows, hrows), 0)
    a_step, a_row = a & 1, (a >> 1) & (pn.rows - 1)
    a_y, a_place = (a >> (1 + lrow)) & (ny - 1), a >> (1 + lrow + ly)
    a_from = a_y * crow + a_row * span_rows + a_place * STEPS + a_step
    turn = jnp.where(iota((hrows, hrows), 1) == a_from, 1.0, 0.0)
    lane = iota((crow, LANES), 1)
    stat = []
    for h in range(halves):
        at = slice(h * crow, (h + 1) * crow)
        rows = [
            jnp.where(
                lane == 0,
                cols[at, nx * ny + y : nx * ny + y + 1],
                jnp.where(lane == 1, cols[at, (nx + 1) * ny + y : (nx + 1) * ny + y + 1], 0.0),
            )
            for y in range(ny)
        ]
        stat.append(mm(turn, jnp.concatenate(rows, axis=0), HIGH))
    szs[...] = jnp.transpose(jnp.concatenate(stat, axis=0))[0:2, :]
    for k in far_first(nz):
        send(szs, szr.at[k - 1], "azs", k - 1, z_dev(k))
    turn = turn.astype(BF16)
    for h in range(halves):
        for kx, ky in reversed(xy_far):
            slot = (kx * ny + ky - 1) * halves + h
            receive(oxr.at[kx, y_of(ny - ky), h], "a", slot, xy_dev(kx, ky))
        at = slice(h * crow, (h + 1) * crow)
        sums = []
        for y in range(ny):
            acc = cols[at, y : y + 1] * oxr[0, y, h].astype(F32)
            for kx in range(1, nx):
                c = kx * ny + y
                acc = acc + cols[at, c : c + 1] * oxr[kx, y, h].astype(F32)
            sums.append(acc.astype(BF16))
        turned = mm(turn, jnp.concatenate(sums, axis=0)).astype(BF16)
        for p in range(per):
            place = h * per + p
            ozs[place] = turned[p * pn.block : (p + 1) * pn.block, :]
            k = zorder[place]
            if k > 0:
                send(ozs.at[place], ozr.at[k - 1], "az", k - 1, z_dev(k))

    receive(ops.at[1 - core], "op", 0, core_dev)
    for z in range(nz):
        for x in range(nx):
            c = z * nx + x
            for half in range(2):
                piece = ops[half, :, c * pn.feat : (c + 1) * pn.feat]
                opw[x, z, half * pn.vrows : (half + 1) * pn.vrows, :] = pad_lanes(
                    piece, pn.featp
                )
    for k in range(1, ne):
        receive(ra.at[e_of(ne - k)], "res", k - 1, e_dev(k))
    lt = log2(pn.tok)

    def owner_of(n):
        y = (n >> lt) & (ny - 1)
        return 2 * y + (n >> (lt + ly)), n & (pn.tok - 1)

    n_row = iota((pn.total, ne * 16), 0)
    n_owner, n_tok = owner_of(n_row)
    spread = iota((pn.total, ne * 16), 1)
    pick = jnp.where(spread == n_owner * 16 + n_tok, 1.0, 0.0).astype(BF16)
    residual = mm(pick, ra[...].reshape(ne * 16, pn.featp))
    vu_copy.wait()

    def stat_of(ref, k):
        at = zorder.index(k) * pn.block
        return pad_lanes(ref[0:2, at : at + pn.block], LANES)

    for k in range(1, nz):
        receive(szr.at[k - 1], "azs", k - 1, z_dev(k))
    stat = [stat_of(szs, 0)] + [stat_of(szr.at[k - 1], k) for k in range(1, nz)]
    coefs, _, _ = joined([s[0:1, :] for s in stat], [s[1:2, :] for s in stat])
    cols = jnp.transpose(pad_rows(jnp.concatenate(coefs, axis=0), LANES))[0 : pn.block, :]
    acc = cols[:, 0:1] * ozs[nz - 1].astype(F32)
    for k in reversed(far_first(nz)):
        receive(ozr.at[k - 1], "az", k - 1, z_dev(k))
        acc = acc + cols[:, k : k + 1] * ozr[k - 1].astype(F32)
    values = mm(acc.astype(BF16), vus[...]).astype(BF16)

    each = nz // pn.parts

    def partner_chunk(h):
        return pl.ds(h * each, each)

    for h in range(pn.parts):
        for k in xorder:
            for p in range(each):
                place = h * each + p
                block = mm(values, opw[x_of(k), z_of(zorder[place])])
                cs[k, place] = block.astype(BF16)
            if k > 0:
                send(
                    cs.at[k, partner_chunk(h)],
                    cr.at[k - 1, partner_chunk(h)],
                    "cx",
                    (k - 1) * pn.parts + h,
                    x_dev(k),
                )
    for h in range(pn.parts):
        for k in range(1, nx):
            receive(
                cr.at[k - 1, partner_chunk(h)], "cx", (k - 1) * pn.parts + h, x_dev(k)
            )
        for p in range(each):
            place = h * each + p
            acc = cs[0, place].astype(F32)
            for i in range(1, nx):
                acc = acc + cr[i - 1, place].astype(F32)
            zs[place] = acc.astype(BF16)
            k = zorder[place]
            if k > 0:
                send(zs.at[place], zr.at[k - 1], "cz", k - 1, z_dev(k))
    acc = zs[nz - 1].astype(F32)
    for k in reversed(far_first(nz)):
        receive(zr.at[k - 1], "cz", k - 1, z_dev(k))
        acc = acc + zr[k - 1].astype(F32)
    ys[...] = acc.astype(BF16)
    for k in far_first(ne):
        send(ys, yr.at[me], "ce", k - 1, e_dev(k))
    yr[me] = ys[...]
    for k in range(1, ne):
        receive(yr.at[e_of(ne - k)], "ce", k - 1, e_dev(k))
    sides = []
    for c in range(2):
        acc = yr[c].astype(F32)
        for y in range(1, ny):
            acc = acc + yr[2 * y + c].astype(F32)
        sides.append(acc)
    hidden = (residual + jnp.concatenate(sides, axis=0)).astype(BF16)
    hidden_f = hidden.astype(F32)

    scaled = (hidden_f[:, 0 : pn.feat] * gain_ref[...].reshape(1, pn.feat)).astype(BF16)
    pltpu.make_async_copy(gus, gus, gu_sem).wait()
    fb = pn.fb
    for h in range(pn.parts):
        for k in xorder:
            for p in range(each):
                place = h * each + p
                block = mm(scaled, gus[x_of(k), z_of(zorder[place])])
                es[k, place] = block.astype(BF16)
            if k > 0:
                send(
                    es.at[k, partner_chunk(h)],
                    exr.at[k - 1, partner_chunk(h)],
                    "ex",
                    (k - 1) * pn.parts + h,
                    x_dev(k),
                )
        if h == 0:
            squares = jnp.sum(hidden_f * hidden_f, axis=1, keepdims=True)
            squares = pad_rows(jnp.broadcast_to(squares, (pn.total, LANES)), LANES)
            qxs[...] = jnp.transpose(squares)[0:2, :]
            for k in far_first(nx):
                send(qxs, qxr.at[k - 1], "sx", k - 1, x_dev(k))
    acc = qxs[...]
    for k in range(1, nx):
        receive(qxr.at[k - 1], "sx", k - 1, x_dev(k))
        acc = acc + qxr[k - 1]
    qzs[...] = acc
    for h in range(pn.parts):
        for k in range(1, nx):
            receive(
                exr.at[k - 1, partner_chunk(h)], "ex", (k - 1) * pn.parts + h, x_dev(k)
            )
        for p in range(each):
            place = h * each + p
            acc = es[0, place].astype(F32)
            for i in range(1, nx):
                acc = acc + exr[i - 1, place].astype(F32)
            ezs[place] = acc.astype(BF16)
            k = zorder[place]
            if k > 0:
                send(ezs.at[place], ezr.at[k - 1], "ez", k - 1, z_dev(k))
                send(qzs, qzr.at[k - 1], "sz", k - 1, z_dev(k))
    acc = qzs[...]
    for k in range(1, nz):
        receive(qzr.at[k - 1], "sz", k - 1, z_dev(k))
        acc = acc + qzr[k - 1]
    scale_row = lax.rsqrt(acc / pn.model + norm_eps)
    scale = jnp.transpose(pad_rows(scale_row, LANES))[0 : pn.total, 0:1]
    acc = ezs[nz - 1].astype(F32)
    for k in reversed(far_first(nz)):
        receive(ezr.at[k - 1], "ez", k - 1, z_dev(k))
        acc = acc + ezr[k - 1].astype(F32)
    acc = acc * scale
    gate, up = acc[:, 0:fb], acc[:, fb : 2 * fb]
    activated = gate / (1.0 + jnp.exp(-gate)) * up
    act[my_x, my_z] = activated.astype(BF16)

    for k in far_first(nz):
        send(act.at[my_x, my_z], act.at[my_x, my_z], "gz", k - 1, z_dev(k))
    dn_copy.wait()
    for k in [0] + list(reversed(far_first(nz))):
        block = act.at[my_x, z_of(nz - k)]
        if k > 0:
            receive(block, "gz", k - 1, z_dev(k))
        for i in far_first(nx):
            send(block, block, "gx", (i - 1) * nz + k, x_dev(i))
    depth = pn.nzz * fb
    outs = [jnp.zeros((pn.total, pn.feat), F32) for _ in range(pn.experts)]
    for k in [0] + list(reversed(far_first(nx))):
        xp = x_of(nx - k)
        if k > 0:
            for i in range(nz):
                receive(act.at[xp, z_of(nz - i)], "gx", (k - 1) * nz + i, x_dev(k))
        for j in range(pn.experts):
            rows = jnp.concatenate(
                [act[xp, j * pn.nzz + zz] for zz in range(pn.nzz)], axis=1
            )
            down = dns[j, :, pl.ds(pl.multiple_of(xp * depth, depth), depth)]
            outs[j] = outs[j] + mm_nt(rows, down)

    s_row = iota((ne * 16, pn.total), 0)
    s_owner, s_tok = owner_of(iota((ne * 16, pn.total), 1))
    acc = jnp.zeros((ne * 16, pn.featp), F32)
    for j in range(pn.experts):
        put = jnp.where(s_row == s_owner * 16 + j * pn.tok + s_tok, 1.0, 0.0).astype(BF16)
        acc = acc + mm(put, pad_lanes(outs[j], pn.featp).astype(BF16))
    fs[...] = acc.astype(BF16).reshape(ne, 16, pn.featp)
    for k in far_first(ne):
        send(fs.at[e_of(k)], fr.at[me], "f", k - 1, e_dev(k))
    fr[me] = fs[me]

    ids = pad_rows(jnp.concatenate([ids_ref[r] for r in range(pn.rows)], axis=0), 8)
    coef = pad_rows(jnp.concatenate([rw_ref[r] for r in range(pn.rows)], axis=0), 8)
    c_row, c_col = iota((8, ne * 16), 0), iota((8, ne * 16), 1)
    place = c_col & 15
    expert = (c_col >> 4) * pn.experts + (place >> lt)
    used = (place < pn.experts * pn.tok) & ((place & (pn.tok - 1)) == c_row)
    mix = jnp.zeros((8, ne * 16), F32)
    for t in range(TOPK):
        mix = mix + jnp.where(used & (expert == ids[:, t : t + 1]), coef[:, t : t + 1], 0.0)
    own_row, own_col = iota((8, pn.total), 0), iota((8, pn.total), 1)
    own_at = core * (pn.total // 2) + my_y * pn.tok + own_row
    own = jnp.where((own_col == own_at) & (own_row < pn.tok), 1.0, 0.0).astype(BF16)
    own_hidden = mm(own, hidden)

    for copy in pending[: 1 - ne]:
        copy.wait_send()
    for k in range(1, ne):
        receive(fr.at[e_of(ne - k)], "f", k - 1, e_dev(k))
    returned = fr[...].reshape(ne * 16, pn.featp).astype(F32)
    mixed = own_hidden + mm(mix, returned, HIGH)
    for r in range(pn.rows):
        out_ref[r] = mixed[r * STEPS : (r + 1) * STEPS, 0 : pn.feat].astype(BF16)
    for copy in pending[1 - ne :]:
        copy.wait_send()


def on_device(
    nx,
    queries,
    new_latent,
    cache,
    lengths,
    value_up,
    out_proj,
    residual,
    norm_gain,
    route_ids,
    route_weights,
    gate_up,
    expert_down,
):
    ne = lax.axis_size("exp")
    nz = lax.axis_size("ctx") // nx
    pn = Plan(nx, nz, ne, queries, cache, out_proj, gate_up)
    keys = pn.span + LANES
    stat_lanes = nz * pn.block
    any_spec = pl.BlockSpec(memory_space=pl.ANY)
    vmem_spec = pl.BlockSpec(memory_space=pltpu.VMEM)
    fp, total = pn.featp, pn.total
    v = pltpu.VMEM
    crow = pn.rows * STEPS * pn.per
    scratch = [
        v(new_latent.shape, BF16),
        pltpu.SMEM(lengths.shape, jnp.int32),
        v(residual.shape, BF16),
        v(norm_gain.shape, F32),
        v(route_ids.shape, jnp.int32),
        v(route_weights.shape, F32),
        v((pn.rows, STEPS, pn.width, pn.heads), BF16),
        v((pn.rows, pn.width, keys), BF16),
        v(value_up.shape[1:], BF16),
        v((2, *out_proj.shape), BF16),
        v((nx, nz, pn.feat, 2 * pn.fb), BF16),
        v((pn.experts, pn.feat, pn.ffe), BF16),
        v((nx, nz, 2 * pn.vrows, fp), BF16),
        v((16, fp), BF16),
        v((ne, 16, fp), BF16),
        v((nx, pn.hl, pn.halves, crow, LATENT), BF16),
        v((nx, pn.ny, pn.halves, crow, LATENT), BF16),
        v((nx, 2, stat_lanes), F32),
        v((nx, pn.ny, 2, stat_lanes), F32),
        v((nz, pn.block, LATENT), BF16),
        v((nz - 1, pn.block, LATENT), BF16),
        v((2, stat_lanes), F32),
        v((nz - 1, 2, stat_lanes), F32),
        v((stat_lanes, LANES), F32),
        v((nx, nz, total // 2, fp), BF16),
        v((nx - 1, nz, total // 2, fp), BF16),
        v((nz, total // 2, fp), BF16),
        v((nz - 1, total // 2, fp), BF16),
        v((total // 2, fp), BF16),
        v((ne, total // 2, fp), BF16),
        v((2, LANES), F32),
        v((nx - 1, 2, LANES), F32),
        v((2, LANES), F32),
        v((nz - 1, 2, LANES), F32),
        v((nx, nz, total, 2 * pn.fb), BF16),
        v((nx - 1, nz, total, 2 * pn.fb), BF16),
        v((nz, total, 2 * pn.fb), BF16),
        v((nz - 1, total, 2 * pn.fb), BF16),
        v((nx, nz, total, pn.fb), BF16),
        v((ne, 16, fp), BF16),
        v((ne, 16, fp), BF16),
        pltpu.SemaphoreType.DMA((pn.n_remote,)),
        pltpu.SemaphoreType.DMA((pn.n_remote,)),
        pltpu.SemaphoreType.DMA((pn.n_local,)),
    ]
    return pl.pallas_call(
        functools.partial(kernel, pn),
        out_shape=jax.ShapeDtypeStruct(residual.shape, BF16),
        in_specs=[any_spec] * 12,
        out_specs=vmem_spec,
        scratch_shapes=scratch,
        compiler_params=pltpu.CompilerParams(
            collective_id=0, has_side_effects=True, vmem_limit_bytes=60 * 1024 * 1024
        ),
        name="decode_layer",
    )(
        jnp.swapaxes(queries, 2, 3),
        new_latent,
        jnp.swapaxes(cache, 1, 2),
        lengths,
        value_up,
        out_proj,
        residual,
        norm_gain,
        route_ids,
        route_weights,
        gate_up,
        jnp.swapaxes(expert_down, 1, 2),
    )


def solution(mesh, nx=CHIPS_X):
    in_specs = (
        P("exp", None, None, None),
        P("exp", None, None),
        P("exp", "ctx", None),
        P("exp"),
        P("ctx", None, None),
        P(("ctx", "exp"), None),
        P("exp", None, "ctx"),
        P("ctx"),
        P("exp", None, None),
        P("exp", None, None),
        P("exp", "ctx", None),
        P("exp", None, "ctx"),
    )
    return jax.shard_map(
        functools.partial(on_device, nx),
        mesh=mesh,
        in_specs=in_specs,
        out_specs=P("exp", None, "ctx"),
        check_vma=False,
    )
```
